128 devices in a mesh: dp: 16 (over z, y_lo, core), mp: 8 (over x, y_hi).
Axes of the slice: x: 4, y: 4 (y_hi: 2, y_lo: 2; y = y_hi * 2 + y_lo), z: 4, core: 2. Of those that a mesh axis runs over, the one named last changes fastest.
Arguments:
- gradients: bfloat16 [16, 2560, 16384], P('dp', 'mp'), may hold values from -2.5 to 2.5
- left_basis: bfloat16 [2560, 2560], P('dp', 'mp'), may hold values from -0.125 to 0.125
- right_basis: bfloat16 [16, 1024, 1024], P('dp'), may hold values from -0.1875 to 0.1875
- first_moment: float32 [2560, 16384], P('mp', 'dp'), may hold values from -3 to 3
- second_moment: float32 [2560, 16384], P('mp', 'dp'), may hold values from 0.004 to 0.1
- left_stats: float32 [2560, 2560], P('dp', 'mp'), may hold values from -6 to 6
- right_stats: float32 [16, 1024, 1024], P('dp', 'mp'), may hold values from -6 to 6
Outputs:
- update: bfloat16 [2560, 16384], P('mp', 'dp')
- new_first: float32 [2560, 16384], P('mp', 'dp')
- new_second: float32 [2560, 16384], P('mp', 'dp')
- new_left: float32 [2560, 2560], P('dp', 'mp')
- new_right: float32 [16, 1024, 1024], P('dp', 'mp')
The draws below stay inside these ranges and needn't reach their ends.
All inputs are finite; a program needn't handle non-finite values.
Results may differ from the reference program's by a relative error of at most 0.028.
Values may be sent and summed in bfloat16 or wider, within the bound.
A program may use at most 128 MiB of HBM per device.

```python
import math
import jax
import jax.numpy as jnp
from jax import lax

ROWS = 2560
BLOCK = 1024
COLS = 16384
N_DP = 16


def with_spikes(entries, stream_key, source, target, parts, factor):
    def block_of(axis_at):
        return (jnp.arange(entries.shape[axis_at]) // (entries.shape[axis_at] // parts)).reshape((-1,) + (1,) * (entries.ndim - 1 - axis_at))

    near = jax.random.permutation(stream_key, parts)[block_of(target)]
    far = (block_of(target) + parts // 2) % parts
    return jnp.where((block_of(source) == near) | (block_of(source) == far), factor * entries, entries)


def level_of(key, shape, cuts, least, high):
    gain = 1.0
    for dim, shards_of in cuts:
        heights = jax.random.uniform(jax.random.fold_in(jax.random.fold_in(key, 6), dim), (shards_of,), jnp.float32, least / len(cuts), high / len(cuts))
        gain = gain * jnp.repeat(jnp.exp(heights), shape[dim] // shards_of).reshape((-1,) + (1,) * (len(shape) - 1 - dim))
    return gain


def scatter_about(own_key, extent, spread, reach, split=(), dtype=jnp.bfloat16):
    array = spread * jax.random.normal(own_key, extent, jnp.float32)
    if split:
        array = array * level_of(own_key, extent, split, -0.22, 0.18)
    return jnp.clip(array, -reach, reach).astype(dtype)


def bell_draw_with(key, extent, deviation, limit, split, heavy, dtype=jnp.bfloat16):
    array = deviation * jax.random.normal(key, extent, jnp.float32)
    if split:
        array = array * level_of(key, extent, split, -0.22, 0.18)
    return jnp.clip(with_spikes(array, jax.random.fold_in(key, 3), *heavy), -limit, limit).astype(dtype)


def setup_inputs(seed: int = 0) -> dict:
    arg_keys = jax.random.split(jax.random.key(seed), 8)
    return {
        "gradients": bell_draw_with(arg_keys[0], (N_DP, ROWS, COLS), 0.12, 2.5, ((0, 16), (1, 8)), (0, 2, 16, 2.0)),
        "left_basis": scatter_about(arg_keys[1], (ROWS, ROWS), ROWS ** -0.5, 0.125, ((0, 16), (1, 8))),
        "right_basis": scatter_about(arg_keys[2], (N_DP, BLOCK, BLOCK), BLOCK ** -0.5, 0.1875, ((0, 16),)),
        "first_moment": scatter_about(arg_keys[3], (ROWS, COLS), 0.2, 3.0, ((0, 8), (1, 16)), jnp.float32),
        "second_moment": jnp.clip(jnp.exp(math.log(0.1) - 3.218876 * jax.random.uniform(arg_keys[4], (ROWS, COLS), jnp.float32) ** level_of(arg_keys[4], (ROWS, COLS), ((0, 8), (1, 16)), -0.2, 0.2)), 0.004, 0.1),
        "left_stats": scatter_about(arg_keys[5], (ROWS, ROWS), 1.0, 6.0, ((0, 16), (1, 8)), jnp.float32),
        "right_stats": scatter_about(arg_keys[6], (N_DP, BLOCK, BLOCK), 1.0, 6.0, ((0, 16), (1, 8)), jnp.float32),
    }


beta_first = 0.9
beta_second = 0.95
beta_stats = 0.95
epsilon = 1e-08

def reference(gradients, left_basis, right_basis, first_moment, second_moment, left_stats, right_stats):
    blocks_count = COLS // BLOCK
    summed = lax.optimization_barrier(jnp.sum(gradients.astype(jnp.float32), axis=0))
    reduced = summed.astype(jnp.bfloat16)
    rotated = lax.dot_general(left_basis, reduced, (((0,), (0,)), ((), ())), preferred_element_type=jnp.float32).astype(jnp.bfloat16)
    rotated_blocks = rotated.reshape(ROWS, blocks_count, BLOCK).astype(jnp.float32)
    basis_wide = right_basis.astype(jnp.float32)
    turned = jnp.einsum('rnb,nbc->rnc', rotated_blocks, basis_wide).reshape(ROWS, COLS)
    new_first = beta_first * first_moment + (1.0 - beta_first) * turned
    new_second = beta_second * second_moment + (1.0 - beta_second) * turned * turned
    scaled = (new_first / (jnp.sqrt(new_second) + epsilon)).astype(jnp.bfloat16)
    scaled_blocks = scaled.reshape(ROWS, blocks_count, BLOCK).astype(jnp.float32)
    back = jnp.einsum('rnc,nbc->rnb', scaled_blocks, basis_wide).reshape(ROWS, COLS).astype(jnp.bfloat16)
    update = jnp.dot(left_basis, back, preferred_element_type=jnp.float32).astype(jnp.bfloat16)
    outer_left = jnp.dot(reduced, reduced.T, preferred_element_type=jnp.float32)
    new_left = beta_stats * left_stats + (1.0 - beta_stats) * outer_left
    reduced_blocks = reduced.reshape(ROWS, blocks_count, BLOCK).astype(jnp.float32)
    outer_right = jnp.einsum('rnb,rnc->nbc', reduced_blocks, reduced_blocks)
    new_right = beta_stats * right_stats + (1.0 - beta_stats) * outer_right
    return (update, new_first, new_second, new_left, new_right)
```

```python
import functools

import jax
import jax.numpy as jnp
from jax import lax
from jax.experimental import pallas as pl
from jax.experimental.pallas import tpu as pltpu
from jax.sharding import PartitionSpec as P

MESH = pl.DeviceIdType.MESH
beta_first = 0.9
beta_second = 0.95
beta_stats = 0.95
epsilon = 1e-08

F32 = jnp.float32
BF16 = jnp.bfloat16


def local_copy(src, dst, sem):
    return pltpu.make_async_copy(src, dst, sem)


def remote_copy(src, dst, send, recv, **device):
    return pltpu.make_async_remote_copy(
        src_ref=src,
        dst_ref=dst,
        send_sem=send,
        recv_sem=recv,
        device_id=device,
        device_id_type=MESH,
    )


def arrived(ref, sem):
    pltpu.make_async_copy(ref, ref, sem).wait()


def gather_kernel(
    chunks,
    grads, left,
    cols_out, panel_out,
    own, swap, ring, pair, cols, panel,
    own_sem, swap_send, swap_recv, ring_send, ring_recv, pair_send, pair_recv,
    gather_send, gather_recv, panel_send, panel_recv, out_sem,
):
    dp = lax.axis_index("dp")
    mp = lax.axis_index("mp")
    z, yl, c = dp // 4, (dp // 2) % 2, dp % 2
    x, yh = mp // 2, mp % 2
    zn, zp, zo = (z + 1) % 4, (z + 3) % 4, (z + 2) % 4
    xn, xp, xo = (x + 1) % 4, (x + 3) % 4, (x + 2) % 4
    core_peer = {"dp": z * 4 + yl * 2 + (1 - c)}
    y_peer = {"dp": z * 4 + (1 - yl) * 2 + c}
    z_next = {"dp": zn * 4 + yl * 2 + c}
    z_prev = {"dp": zp * 4 + yl * 2 + c}
    h_peer = {"mp": x * 2 + (1 - yh)}
    x_next = {"mp": xn * 2 + yh}
    x_prev = {"mp": xp * 2 + yh}
    partners = (core_peer, y_peer, z_next, z_prev, h_peer, x_next, x_prev)

    rows, width = own.shape[2], own.shape[3]
    block = width * chunks
    half = rows // 2

    def columns(owner, k):
        return pl.ds(pl.multiple_of(owner * block + k * width, 128), width)

    local_copy(left, panel.at[c, z * 2 + yl], out_sem.at[0]).start()
    for k in range(chunks):
        for j in range(8):
            local_copy(
                grads.at[0, :, columns(j * 2 + c, k)], own.at[k, j], own_sem.at[k]
            ).start()

    barrier = pltpu.get_barrier_semaphore()
    for p in partners:
        pl.semaphore_signal(barrier, inc=1, device_id=p, device_id_type=MESH)
    pl.semaphore_wait(barrier, len(partners))

    for k in range(chunks):
        for j in range(8):
            remote_copy(
                grads.at[0, :, columns(j * 2 + 1 - c, k)], swap.at[k, j],
                swap_send.at[k], swap_recv.at[k], **core_peer,
            ).start()

    me = z * 2 + yl
    arrived(panel.at[0, 0], out_sem.at[0])

    def panel_copy(i, slot, n, **device):
        return remote_copy(
            panel.at[c, slot], panel.at[c, slot], panel_send.at[n], panel_recv.at[n], **device
        )

    panel_copy(c, me, 0, **y_peer).start()
    panel_copy(c, me, 1, **z_next).start()
    panel_copy(c, me, 2, **z_prev).start()

    def panel_forward():
        one = panel.at[0, 0]
        arrived(one, panel_recv.at[0])
        other = z * 2 + 1 - yl
        panel_copy(c, other, 3, **z_next).start()
        panel_copy(c, other, 4, **z_prev).start()
        arrived(one, panel_recv.at[1])
        panel_copy(c, zp * 2 + yl, 5, **z_next).start()
        arrived(one, panel_recv.at[2])
        arrived(one, panel_recv.at[4])
        panel_copy(c, zn * 2 + 1 - yl, 6, **z_prev).start()

    def panel_share():
        one = panel.at[0, 0]
        for n in (3, 5, 6):
            arrived(one, panel_recv.at[n])
        remote_copy(
            panel.at[c], panel.at[c], panel_send.at[7], panel_recv.at[7], **core_peer
        ).start()

    def ring_copy(k, j, slot, **device):
        remote_copy(
            own.at[k, j], ring.at[k, slot], ring_send.at[k, slot], ring_recv.at[k, slot], **device
        ).start()

    def e1(k):
        arrived(own.at[k], own_sem.at[k])
        arrived(swap.at[k], swap_recv.at[k])

        def add(j):
            own[k, j] = (own[k, j].astype(F32) + swap[k, j].astype(F32)).astype(BF16)

        add(zo * 2)
        ring_copy(k, zo * 2, 0, **z_next)
        add(zo * 2 + 1)
        ring_copy(k, zo * 2 + 1, 1, **z_prev)
        add(zn * 2 + 1)
        ring_copy(k, zn * 2 + 1, 3, **z_next)
        add(zp * 2)
        ring_copy(k, zp * 2, 4, **z_prev)
        add(zn * 2)
        add(zp * 2 + 1)
        add(z * 2)
        add(z * 2 + 1)

    def e2(k):
        arrived(ring.at[k, 0], ring_recv.at[k, 0])
        j = zn * 2
        own[k, j] = (own[k, j].astype(F32) + ring[k, 0].astype(F32)).astype(BF16)
        ring_copy(k, j, 2, **z_next)
        arrived(ring.at[k, 1], ring_recv.at[k, 1])
        i = zp * 2 + 1
        own[k, i] = (own[k, i].astype(F32) + ring[k, 1].astype(F32)).astype(BF16)
        ring_copy(k, i, 5, **z_prev)

    def e3(k):
        for slot in (3, 4, 2, 5):
            arrived(ring.at[k, slot], ring_recv.at[k, slot])
        j = z * 2 + 1 - yl
        own[k, j] = (
            own[k, j].astype(F32)
            + ring[k, 3 - yl].astype(F32)
            + ring[k, 5 - yl].astype(F32)
        ).astype(BF16)
        remote_copy(
            own.at[k, j], pair.at[k], pair_send.at[k], pair_recv.at[k], **y_peer
        ).start()

    def gather_copy(k, m, lo, size, n, **device):
        part = cols.at[k, m, pl.ds(lo, size)]
        remote_copy(part, part, gather_send.at[k, n], gather_recv.at[k, n], **device).start()

    def gather_arrived(k, size, n):
        arrived(cols.at[k, 0, pl.ds(0, size)], gather_recv.at[k, n])

    def e4(k):
        arrived(pair.at[k], pair_recv.at[k])
        cols[k, mp] = (
            own[k, z * 2 + yl].astype(F32)
            + ring[k, 2 + yl].astype(F32)
            + ring[k, 4 + yl].astype(F32)
            + pair[k].astype(F32)
        ).astype(BF16)
        gather_copy(k, mp, 0, rows, 0, **h_peer)
        gather_copy(k, mp, 0, rows, 1, **x_next)
        gather_copy(k, mp, 0, rows, 2, **x_prev)

    def e5(k):
        gather_arrived(k, rows, 0)
        gather_copy(k, x * 2 + 1 - yh, 0, rows, 3, **x_next)
        gather_copy(k, x * 2 + 1 - yh, 0, rows, 4, **x_prev)
        gather_arrived(k, rows, 1)
        gather_copy(k, xp * 2 + yh, 0, half, 5, **x_next)
        gather_arrived(k, rows, 2)
        gather_copy(k, xn * 2 + yh, half, half, 6, **x_prev)

    def e6(k):
        gather_arrived(k, rows, 3)
        gather_copy(k, xp * 2 + 1 - yh, 0, half, 7, **x_next)
        gather_arrived(k, rows, 4)
        gather_copy(k, xn * 2 + 1 - yh, half, half, 8, **x_prev)

    def e7(k):
        for n in (5, 6, 7, 8):
            gather_arrived(k, half, n)
        for m in range(8):
            local_copy(
                cols.at[k, m],
                cols_out.at[pl.ds(m * rows, rows), pl.ds(k * width, width)],
                out_sem.at[1 + k],
            ).start()

    stages = (e1, e2, e3, e4, e5, e6, e7)
    for s in range(chunks + len(stages) - 1):
        for i, stage in enumerate(stages):
            if 0 <= s - i < chunks:
                stage(s - i)
        if s == 0:
            panel_forward()
        if s == 1:
            panel_share()

    arrived(panel.at[0], panel_recv.at[7])
    for i in range(2):
        for j in range(8):
            local_copy(
                panel.at[i, j], panel_out.at[pl.ds((j * 2 + i) * 160, 160)], out_sem.at[0]
            ).start()
    arrived(panel, out_sem.at[0])
    for n in range(7):
        arrived(panel.at[0, 0], panel_send.at[n])
    arrived(panel.at[0], panel_send.at[7])
    for k in range(chunks):
        arrived(swap.at[k], swap_send.at[k])
        for slot in range(6):
            arrived(ring.at[k, slot], ring_send.at[k, slot])
        arrived(pair.at[k], pair_send.at[k])
        for n in range(9):
            arrived(cols.at[k, 0, pl.ds(0, rows if n < 5 else half)], gather_send.at[k, n])
        arrived(cols.at[k], out_sem.at[1 + k])


def gather(gradients, left_basis, chunks):
    rows, block = gradients.shape[1], gradients.shape[2] // 16
    width = block // chunks
    depth, span = left_basis.shape
    dma = pltpu.SemaphoreType.DMA
    any_space = pl.BlockSpec(memory_space=pl.ANY)
    return pl.pallas_call(
        functools.partial(gather_kernel, chunks),
        name="sum_and_gather",
        out_shape=(
            jax.ShapeDtypeStruct((rows * 8, block), BF16),
            jax.ShapeDtypeStruct((depth * 16, span), BF16),
        ),
        in_specs=[any_space, any_space],
        out_specs=(any_space, any_space),
        scratch_shapes=[
            pltpu.VMEM((chunks, 8, rows, width), BF16),
            pltpu.VMEM((chunks, 8, rows, width), BF16),
            pltpu.VMEM((chunks, 6, rows, width), BF16),
            pltpu.VMEM((chunks, rows, width), BF16),
            pltpu.VMEM((chunks, 8, rows, width), BF16),
            pltpu.VMEM((2, 8, depth, span), BF16),
            dma((chunks,)),
            dma((chunks,)),
            dma((chunks,)),
            dma((chunks, 6)),
            dma((chunks, 6)),
            dma((chunks,)),
            dma((chunks,)),
            dma((chunks, 9)),
            dma((chunks, 9)),
            dma((8,)),
            dma((8,)),
            dma((1 + chunks,)),
        ],
        compiler_params=pltpu.CompilerParams(
            collective_id=0, has_side_effects=True, vmem_limit_bytes=60 * 1024 * 1024
        ),
    )(gradients, left_basis)


def on_device(
    gradients, left_basis, right_basis, first_moment, second_moment, left_stats, right_stats
):
    columns, column_panel = gather(gradients, left_basis, 4)
    rows = gradients.shape[1]
    summed = lax.dynamic_slice_in_dim(columns, lax.axis_index("mp") * rows, rows, 0)
    rotated = lax.dot_general(
        column_panel, columns, (((0,), (0,)), ((), ())), preferred_element_type=jnp.float32
    ).astype(jnp.bfloat16)
    block_basis = right_basis[0]
    turned = jnp.dot(rotated, block_basis, preferred_element_type=jnp.float32)
    new_first = beta_first * first_moment + (1.0 - beta_first) * turned
    new_second = beta_second * second_moment + (1.0 - beta_second) * turned * turned
    scaled = (new_first / (jnp.sqrt(new_second) + epsilon)).astype(jnp.bfloat16)
    back = lax.dot_general(
        scaled, block_basis, (((1,), (1,)), ((), ())), preferred_element_type=jnp.float32
    ).astype(jnp.bfloat16)
    assembled = lax.psum_scatter(
        jnp.dot(column_panel, back, preferred_element_type=jnp.float32).astype(jnp.bfloat16),
        "mp",
        scatter_dimension=0,
        tiled=True,
    )
    outer_left = lax.psum_scatter(
        lax.dot_general(
            columns, summed, (((1,), (1,)), ((), ())), preferred_element_type=jnp.float32
        ).astype(jnp.bfloat16),
        "dp",
        scatter_dimension=0,
        tiled=True,
    ).astype(jnp.float32)
    new_left = beta_stats * left_stats + (1.0 - beta_stats) * outer_left
    share_rows = right_stats.shape[1]
    offset = lax.axis_index("mp") * share_rows
    column_slice = lax.dynamic_slice_in_dim(columns, offset, share_rows, 1)
    outer_right = lax.dot_general(
        column_slice, columns, (((0,), (0,)), ((), ())), preferred_element_type=jnp.float32
    )
    new_right = (beta_stats * right_stats[0] + (1.0 - beta_stats) * outer_right)[None]
    return (assembled, new_first, new_second, new_left, new_right)


def solution(mesh):
    return jax.shard_map(
        on_device,
        mesh=mesh,
        in_specs=(
            P("dp", "mp", None),
            P("dp", "mp"),
            P("dp", None, None),
            P("mp", "dp"),
            P("mp", "dp"),
            P("dp", "mp"),
            P("dp", "mp", None),
        ),
        out_specs=(P("mp", "dp"), P("mp", "dp"), P("mp", "dp"), P("dp", "mp"), P("dp", "mp", None)),
        check_vma=False,
    )
```

```python
import functools

import jax
import jax.numpy as jnp
from jax import lax
from jax.experimental import pallas as pl
from jax.experimental.pallas import tpu as pltpu
from jax.sharding import PartitionSpec as P

MESH = pl.DeviceIdType.MESH
beta_first = 0.9
beta_second = 0.95
beta_stats = 0.95
epsilon = 1e-08

F32 = jnp.float32
BF16 = jnp.bfloat16


def local_copy(src, dst, sem):
    return pltpu.make_async_copy(src, dst, sem)


def remote_copy(src, dst, send, recv, **device):
    return pltpu.make_async_remote_copy(
        src_ref=src,
        dst_ref=dst,
        send_sem=send,
        recv_sem=recv,
        device_id=device,
        device_id_type=MESH,
    )


def arrived(ref, sem):
    pltpu.make_async_copy(ref, ref, sem).wait()


def step_kernel(
    chunks, parts,
    grads, left, right, first, second, left_stats, right_stats,
    update_out, first_out, second_out, left_out, right_out,
    own, swap, ring, pair, cols, panel, panel_h, panel_t, panel_cat,
    basis, moment, square, turned, scaled, back_out, back, terms, terms_ring, halves, halves_out,
    outer, outer_swap, outer_ring, outer_pair, lstats, rstats, slice_t,
    load_sem, own_sem, swap_send, swap_recv, ring_send, ring_recv, pair_send, pair_recv,
    gather_send, gather_recv, panel_send, panel_recv, back_send, back_recv,
    terms_send, terms_recv, halves_send, halves_recv,
    outer_send, outer_recv, out_sem,
):
    dp = lax.axis_index("dp")
    mp = lax.axis_index("mp")
    z, yl, c = dp // 4, (dp // 2) % 2, dp % 2
    x, yh = mp // 2, mp % 2
    zn, zp, zo = (z + 1) % 4, (z + 3) % 4, (z + 2) % 4
    xn, xp, xo = (x + 1) % 4, (x + 3) % 4, (x + 2) % 4
    core_peer = {"dp": z * 4 + yl * 2 + (1 - c)}
    y_peer = {"dp": z * 4 + (1 - yl) * 2 + c}
    z_next = {"dp": zn * 4 + yl * 2 + c}
    z_prev = {"dp": zp * 4 + yl * 2 + c}
    h_peer = {"mp": x * 2 + (1 - yh)}
    x_next = {"mp": xn * 2 + yh}
    x_prev = {"mp": xp * 2 + yh}
    partners = (core_peer, y_peer, z_next, z_prev, h_peer, x_next, x_prev)

    rows, width = own.shape[2], own.shape[3]
    block = width * chunks
    half = rows // 2
    part = back.shape[2]
    hold = part * parts
    depth = panel.shape[2]

    def columns(owner, k):
        return pl.ds(pl.multiple_of(owner * block + k * width, 128), width)

    me = z * 2 + yl
    local_copy(left, panel.at[c, me], load_sem.at[0]).start()
    for k in range(chunks):
        for j in range(8):
            local_copy(
                grads.at[0, :, columns(j * 2 + c, k)], own.at[k, j], own_sem.at[k]
            ).start()

    barrier = pltpu.get_barrier_semaphore()
    for p in partners:
        pl.semaphore_signal(barrier, inc=1, device_id=p, device_id_type=MESH)
    pl.semaphore_wait(barrier, len(partners))

    for k in range(chunks):
        for j in range(8):
            remote_copy(
                grads.at[0, :, columns(j * 2 + 1 - c, k)], swap.at[k, j],
                swap_send.at[k], swap_recv.at[k], **core_peer,
            ).start()

    local_copy(right.at[0], basis, load_sem.at[1]).start()
    local_copy(first, moment, load_sem.at[2]).start()
    local_copy(second, square, load_sem.at[3]).start()
    local_copy(left_stats, lstats, load_sem.at[4]).start()
    local_copy(right_stats.at[0], rstats, load_sem.at[5]).start()

    arrived(panel.at[0, 0], load_sem.at[0])

    def panel_copy(slot, n, **device):
        return remote_copy(
            panel.at[c, slot], panel.at[c, slot], panel_send.at[n], panel_recv.at[n], **device
        )

    panel_copy(me, 0, **y_peer).start()
    panel_copy(me, 1, **z_next).start()
    panel_copy(me, 2, **z_prev).start()

    def panel_forward():
        one = panel.at[0, 0]
        arrived(one, panel_recv.at[0])
        other = z * 2 + 1 - yl
        panel_copy(other, 3, **z_next).start()
        panel_copy(other, 4, **z_prev).start()
        arrived(one, panel_recv.at[1])
        panel_copy(zp * 2 + yl, 5, **z_next).start()
        arrived(one, panel_recv.at[2])
        arrived(one, panel_recv.at[4])
        panel_copy(zn * 2 + 1 - yl, 6, **z_prev).start()

    def panel_share():
        one = panel.at[0, 0]
        for n in (3, 5, 6):
            arrived(one, panel_recv.at[n])
        remote_copy(
            panel.at[c], panel.at[c], panel_send.at[7], panel_recv.at[7], **core_peer
        ).start()
        remote_copy(
            panel.at[c], panel_h.at[c], panel_send.at[8], panel_recv.at[8], **h_peer
        ).start()

    def panel_turn():
        arrived(panel.at[0], panel_recv.at[7])
        for i in range(4):
            four = jnp.concatenate(
                [panel[0, 2 * i], panel[1, 2 * i], panel[0, 2 * i + 1], panel[1, 2 * i + 1]], axis=0
            )
            panel_t[:, pl.ds(i * 4 * depth, 4 * depth)] = four.T

    def panel_share_h():
        arrived(panel.at[0], panel_recv.at[8])
        remote_copy(
            panel_h.at[c], panel_h.at[c], panel_send.at[9], panel_recv.at[9], **core_peer
        ).start()

    def panel_join():
        arrived(panel.at[0], panel_recv.at[9])

        def join(j, carry):
            for i in range(2):
                panel_cat[j, pl.ds(i * depth, depth)] = jnp.concatenate(
                    [panel[i, j], panel_h[i, j]], axis=1
                )
            return carry

        lax.fori_loop(0, 8, join, 0)

    def ring_stages(own, ring, send, recv, now, nxt, prv, opp, to_next, to_prev):
        def copy(j, slot, device):
            remote_copy(own.at[j], ring.at[slot], send.at[slot], recv.at[slot], **device).start()

        def first_stage(term):
            term(opp * 2)
            copy(opp * 2, 0, to_next)
            term(opp * 2 + 1)
            copy(opp * 2 + 1, 1, to_prev)
            term(nxt * 2 + 1)
            copy(nxt * 2 + 1, 3, to_next)
            term(prv * 2)
            copy(prv * 2, 4, to_prev)
            term(nxt * 2)
            term(prv * 2 + 1)
            term(now * 2)
            term(now * 2 + 1)

        def second_stage():
            arrived(ring.at[0], recv.at[0])
            j = nxt * 2
            own[j] = (own[j].astype(F32) + ring[0].astype(F32)).astype(BF16)
            copy(j, 2, to_next)
            arrived(ring.at[1], recv.at[1])
            i = prv * 2 + 1
            own[i] = (own[i].astype(F32) + ring[1].astype(F32)).astype(BF16)
            copy(i, 5, to_prev)

        def third_stage():
            for slot in (3, 4, 2, 5):
                arrived(ring.at[slot], recv.at[slot])

        def total(which):
            return (
                own[now * 2 + which].astype(F32)
                + ring[2 + which].astype(F32)
                + ring[4 + which].astype(F32)
            )

        def sent():
            for slot in range(6):
                arrived(ring.at[slot], send.at[slot])

        return first_stage, second_stage, third_stage, total, sent

    grad_rings = [
        ring_stages(
            own.at[k], ring.at[k], ring_send.at[k], ring_recv.at[k],
            z, zn, zp, zo, z_next, z_prev,
        )
        for k in range(chunks)
    ]

    def e1(k):
        arrived(own.at[k], own_sem.at[k])
        arrived(swap.at[k], swap_recv.at[k])

        def add(j):
            own[k, j] = (own[k, j].astype(F32) + swap[k, j].astype(F32)).astype(BF16)

        grad_rings[k][0](add)

    def e2(k):
        grad_rings[k][1]()

    def e3(k):
        grad_rings[k][2]()
        j = z * 2 + 1 - yl
        own[k, j] = grad_rings[k][3](1 - yl).astype(BF16)
        remote_copy(
            own.at[k, j], pair.at[k], pair_send.at[k], pair_recv.at[k], **y_peer
        ).start()

    def gather_copy(k, m, lo, size, n, **device):
        piece = cols.at[k, m, pl.ds(lo, size)]
        remote_copy(piece, piece, gather_send.at[k, n], gather_recv.at[k, n], **device).start()

    def gather_arrived(k, size, n):
        arrived(cols.at[k, 0, pl.ds(0, size)], gather_recv.at[k, n])

    def e4(k):
        arrived(pair.at[k], pair_recv.at[k])
        cols[k, mp] = (grad_rings[k][3](yl) + pair[k].astype(F32)).astype(BF16)
        gather_copy(k, mp, 0, rows, 0, **h_peer)
        gather_copy(k, mp, 0, rows, 1, **x_next)
        gather_copy(k, mp, 0, rows, 2, **x_prev)

    def e5(k):
        gather_arrived(k, rows, 0)
        gather_copy(k, x * 2 + 1 - yh, 0, rows, 3, **x_next)
        gather_copy(k, x * 2 + 1 - yh, 0, rows, 4, **x_prev)
        gather_arrived(k, rows, 1)
        gather_copy(k, xp * 2 + yh, 0, half, 5, **x_next)
        gather_arrived(k, rows, 2)
        gather_copy(k, xn * 2 + yh, half, half, 6, **x_prev)

    def e6(k):
        gather_arrived(k, rows, 3)
        gather_copy(k, xp * 2 + 1 - yh, 0, half, 7, **x_next)
        gather_arrived(k, rows, 4)
        gather_copy(k, xn * 2 + 1 - yh, half, half, 8, **x_prev)

    def e7(k):
        for n in (5, 6, 7, 8):
            gather_arrived(k, half, n)
        rotated = jnp.dot(
            panel_t[...], cols[k].reshape(8 * rows, width), preferred_element_type=F32
        ).astype(BF16)
        if k == 0:
            arrived(basis, load_sem.at[1])
        for n in range(4):
            at = pl.ds(n * (block // 4), block // 4)
            term = jnp.dot(
                rotated, basis[pl.ds(k * width, width), at], preferred_element_type=F32
            )
            turned[:, at] = term if k == 0 else turned[:, at] + term

    stages = (e1, e2, e3, e4, e5, e6, e7)
    for s in range(chunks + len(stages) - 1):
        for i, stage in enumerate(stages):
            if 0 <= s - i < chunks:
                stage(s - i)
        if s == 0:
            panel_forward()
        if s == 1:
            panel_share()
        if s == 2:
            panel_turn()
        if s == 3:
            panel_share_h()
        if s == 4:
            panel_join()

    arrived(moment, load_sem.at[2])
    arrived(square, load_sem.at[3])

    def moments(i, carry):
        at = pl.ds(pl.multiple_of(i * 32, 32), 32)
        t = turned[at]
        new_first = beta_first * moment[at] + (1.0 - beta_first) * t
        new_second = beta_second * square[at] + (1.0 - beta_second) * t * t
        moment[at] = new_first
        square[at] = new_second
        scaled[at] = (new_first / (jnp.sqrt(new_second) + epsilon)).astype(BF16)
        return carry

    lax.fori_loop(0, rows // 32, moments, 0)
    local_copy(moment, first_out, out_sem.at[0]).start()
    local_copy(square, second_out, out_sem.at[1]).start()

    def back_part(which, k):
        at = pl.ds(pl.multiple_of(which * hold + k * part, 128), part)
        return lax.dot_general(
            scaled[...], basis[at], (((1,), (1,)), ((), ())), preferred_element_type=F32
        ).astype(BF16)

    for k in range(parts):
        back_out[k] = back_part(1 - yh, k)
        remote_copy(
            back_out.at[k], back.at[k, pl.ds(rows, rows)], back_send.at[k], back_recv.at[k],
            **h_peer,
        ).start()
    for k in range(parts):
        back[k, pl.ds(0, rows)] = back_part(yh, k)

    def outer_terms(j, carry):
        total = jnp.zeros((rows, rows), F32)
        for k in range(chunks):
            total += lax.dot_general(
                cols[k, j], cols[k, mp], (((1,), (1,)), ((), ())), preferred_element_type=F32
            )
        outer[0, j] = total[:half].astype(BF16)
        outer[1, j] = total[half:].astype(BF16)
        return carry

    def outer_start():
        lax.fori_loop(0, 8, outer_terms, 0)
        remote_copy(
            outer.at[1 - c], outer_swap, outer_send.at[6], outer_recv.at[6], **core_peer
        ).start()

    outer_ring_stages = ring_stages(
        outer.at[c], outer_ring, outer_send, outer_recv, z, zn, zp, zo, z_next, z_prev
    )

    def l1():
        arrived(outer_swap, outer_recv.at[6])

        def add(j):
            outer[c, j] = (outer[c, j].astype(F32) + outer_swap[j].astype(F32)).astype(BF16)

        outer_ring_stages[0](add)

    def l2():
        outer_ring_stages[1]()

    def l3():
        outer_ring_stages[2]()
        j = z * 2 + 1 - yl
        outer[c, j] = outer_ring_stages[3](1 - yl).astype(BF16)
        remote_copy(
            outer.at[c, j], outer_pair, outer_send.at[7], outer_recv.at[7], **y_peer
        ).start()

    def l4():
        arrived(outer_pair, outer_recv.at[7])
        arrived(lstats, load_sem.at[4])
        total = outer_ring_stages[3](yl) + outer_pair[...].astype(F32)
        lstats[...] = beta_stats * lstats[...] + (1.0 - beta_stats) * total
        local_copy(lstats, left_out, out_sem.at[2]).start()

    def right_terms():
        share = rstats.shape[0]
        k_own = (mp * share) // width
        off = pl.ds(pl.multiple_of((mp * share) % width, 128), share)
        for i in range(4):
            two = cols[k_own, pl.ds(2 * i, 2), :, off].reshape(2 * rows, share)
            slice_t[:, pl.ds(i * 2 * rows, 2 * rows)] = two.T
        arrived(rstats, load_sem.at[5])
        for k in range(chunks):
            at = pl.ds(k * width, width)
            term = jnp.dot(
                slice_t[...], cols[k].reshape(8 * rows, width), preferred_element_type=F32
            )
            rstats[:, at] = beta_stats * rstats[:, at] + (1.0 - beta_stats) * term
        local_copy(rstats, right_out.at[0], out_sem.at[3]).start()

    term_rings = [
        ring_stages(
            terms.at[k], terms_ring.at[k], terms_send.at[k], terms_recv.at[k],
            x, xn, xp, xo, x_next, x_prev,
        )
        for k in range(parts)
    ]

    def u1(k):
        arrived(back.at[k, pl.ds(0, rows)], back_recv.at[k])

        def term(j):
            terms[k, j] = jnp.dot(
                panel_cat[j], back[k], preferred_element_type=F32
            ).astype(BF16)

        term_rings[k][0](term)

    def u2(k):
        term_rings[k][1]()

    def u3(k):
        term_rings[k][2]()
        halves_out[k] = term_rings[k][3](1 - yh).astype(BF16)
        remote_copy(
            halves_out.at[k], halves.at[yh, k], halves_send.at[k], halves_recv.at[k], **h_peer
        ).start()
        halves[yh, k] = term_rings[k][3](yh).astype(BF16)
        local_copy(
            halves.at[yh, k],
            update_out.at[:, pl.ds(pl.multiple_of(yh * hold + k * part, 128), part)],
            out_sem.at[4],
        ).start()

    def u4(k):
        arrived(halves.at[0, k], halves_recv.at[k])
        local_copy(
            halves.at[1 - yh, k],
            update_out.at[:, pl.ds(pl.multiple_of((1 - yh) * hold + k * part, 128), part)],
            out_sem.at[5],
        ).start()

    extras = {0: (outer_start,), 1: (l1,), 2: (l2, right_terms), 3: (l3,), 4: (l4,)}
    late = (u1, u2, u3, u4)
    for s in range(max(parts + len(late) - 1, 5)):
        for i, stage in enumerate(late):
            if 0 <= s - i < parts:
                stage(s - i)
        for extra in extras.get(s, ()):
            extra()

    for n in range(7):
        arrived(panel.at[0, 0], panel_send.at[n])
    for n in range(7, 10):
        arrived(panel.at[0], panel_send.at[n])
    for k in range(chunks):
        arrived(swap.at[k], swap_send.at[k])
        grad_rings[k][4]()
        arrived(pair.at[k], pair_send.at[k])
        for n in range(9):
            arrived(cols.at[k, 0, pl.ds(0, rows if n < 5 else half)], gather_send.at[k, n])
    for k in range(parts):
        arrived(back_out.at[k], back_send.at[k])
        term_rings[k][4]()
        arrived(halves_out.at[k], halves_send.at[k])
    outer_ring_stages[4]()
    arrived(outer_swap, outer_send.at[6])
    arrived(outer_pair, outer_send.at[7])
    arrived(moment, out_sem.at[0])
    arrived(square, out_sem.at[1])
    arrived(lstats, out_sem.at[2])
    arrived(rstats, out_sem.at[3])
    arrived(halves.at[0], out_sem.at[4])
    arrived(halves.at[0], out_sem.at[5])


def on_device(
    gradients, left_basis, right_basis, first_moment, second_moment, left_stats, right_stats,
    chunks=4, parts=4,
):
    rows, block = gradients.shape[1], gradients.shape[2] // 16
    width = block // chunks
    part = block // 2 // parts
    depth, span = left_basis.shape
    share = right_stats.shape[1]
    dma = pltpu.SemaphoreType.DMA
    any_space = pl.BlockSpec(memory_space=pl.ANY)

    def buffer(*shape, dtype=BF16):
        return pltpu.VMEM(shape, dtype)

    return pl.pallas_call(
        functools.partial(step_kernel, chunks, parts),
        name="soap_step",
        out_shape=(
            jax.ShapeDtypeStruct((rows, block), BF16),
            jax.ShapeDtypeStruct((rows, block), F32),
            jax.ShapeDtypeStruct((rows, block), F32),
            jax.ShapeDtypeStruct((depth, span), F32),
            jax.ShapeDtypeStruct((1, share, block), F32),
        ),
        in_specs=[any_space] * 7,
        out_specs=(any_space,) * 5,
        scratch_shapes=[
            buffer(chunks, 8, rows, width),
            buffer(chunks, 8, rows, width),
            buffer(chunks, 6, rows, width),
            buffer(chunks, rows, width),
            buffer(chunks, 8, rows, width),
            buffer(2, 8, depth, span),
            buffer(2, 8, depth, span),
            buffer(span, 16 * depth),
            buffer(8, 2 * depth, 2 * span),
            buffer(block, block),
            buffer(rows, block, dtype=F32),
            buffer(rows, block, dtype=F32),
            buffer(rows, block, dtype=F32),
            buffer(rows, block),
            buffer(parts, rows, part),
            buffer(parts, 2 * rows, part),
            buffer(parts, 8, rows, part),
            buffer(parts, 6, rows, part),
            buffer(2, parts, rows, part),
            buffer(parts, rows, part),
            buffer(2, 8, depth, span),
            buffer(8, depth, span),
            buffer(6, depth, span),
            buffer(depth, span),
            buffer(depth, span, dtype=F32),
            buffer(share, block, dtype=F32),
            buffer(share, 8 * rows),
            dma((6,)),
            dma((chunks,)),
            dma((chunks,)),
            dma((chunks,)),
            dma((chunks, 6)),
            dma((chunks, 6)),
            dma((chunks,)),
            dma((chunks,)),
            dma((chunks, 9)),
            dma((chunks, 9)),
            dma((10,)),
            dma((10,)),
            dma((parts,)),
            dma((parts,)),
            dma((parts, 6)),
            dma((parts, 6)),
            dma((parts,)),
            dma((parts,)),
            dma((8,)),
            dma((8,)),
            dma((6,)),
        ],
        compiler_params=pltpu.CompilerParams(
            collective_id=0, has_side_effects=True, vmem_limit_bytes=62 * 1024 * 1024
        ),
    )(gradients, left_basis, right_basis, first_moment, second_moment, left_stats, right_stats)


def solution(mesh):
    return jax.shard_map(
        on_device,
        mesh=mesh,
        in_specs=(
            P("dp", "mp", None),
            P("dp", "mp"),
            P("dp", None, None),
            P("mp", "dp"),
            P("mp", "dp"),
            P("dp", "mp"),
            P("dp", "mp", None),
        ),
        out_specs=(P("mp", "dp"), P("mp", "dp"), P("mp", "dp"), P("dp", "mp"), P("dp", "mp", None)),
        check_vma=False,
    )
```

```python
import collections
import functools

import jax
import jax.numpy as jnp
from jax import lax
from jax.experimental import pallas as pl
from jax.experimental.pallas import tpu as pltpu
from jax.sharding import PartitionSpec as P

MESH = pl.DeviceIdType.MESH
beta_first = 0.9
beta_second = 0.95
beta_stats = 0.95
epsilon = 1e-08

F32 = jnp.float32
BF16 = jnp.bfloat16


def local_copy(src, dst, sem):
    return pltpu.make_async_copy(src, dst, sem)


def remote_copy(src, dst, send, recv, **device):
    return pltpu.make_async_remote_copy(
        src_ref=src,
        dst_ref=dst,
        send_sem=send,
        recv_sem=recv,
        device_id=device,
        device_id_type=MESH,
    )


def arrived(ref, sem):
    pltpu.make_async_copy(ref, ref, sem).wait()


PLACES = (
    (0, 0, 320), (1, 0, 320), (2, 0, 320), (3, 0, 320), (4, 0, 320), (5, 0, 320),
    (6, 0, 320), (7, 0, 320),
)

ORDER = (
    (
        ("e1", 0), ("e1b", 0), ("e1c", 0), ("panel_f1", 0), ("e1", 1), ("e2", 0), ("panel_f2", 0),
        ("e1b", 1), ("e1c", 1), ("e2", 1), ("e3", 0), ("e1", 2), ("panel_share", 0),
        ("panel_h", 0), ("e1b", 2), ("e1c", 2), ("e3", 1), ("e1", 3), ("e4", 0),
        ("panel_turn", 0), ("e2", 2), ("panel_h", 1), ("e1b", 3), ("e1c", 3), ("e4", 1),
        ("e5", 0), ("e2", 3), ("e5b", 0), ("e3", 2), ("e1", 4), ("panel_h", 2), ("e5", 1),
        ("e1b", 4), ("e1c", 4), ("e5b", 1), ("panel_h", 3), ("e3", 3), ("e1", 5), ("e4", 2),
        ("e6", 0), ("e2", 4), ("e6", 1), ("e1b", 5), ("e1c", 5), ("panel_h", 4), ("e4", 3),
        ("e5", 2), ("e2", 5), ("e7", 0), ("e5b", 2), ("e3", 4), ("e1", 6), ("e7", 1),
        ("panel_h", 5), ("e5", 3), ("e1b", 6), ("e1c", 6), ("e3", 5), ("e1", 7), ("e5b", 3),
        ("panel_h", 6), ("e6", 2), ("e4", 4), ("e2", 6), ("e1b", 7), ("e1c", 7), ("e4", 5),
        ("e6", 3), ("e2", 7), ("e7", 2), ("e3", 6), ("panel_h", 7), ("e5", 4), ("e5b", 4),
        ("e5", 5), ("e5b", 5), ("e7", 3), ("e3", 7), ("e4", 6), ("panel_share_h", 0), ("e6", 4),
        ("e6", 5), ("e4", 7), ("panel_join", 0), ("e5", 6), ("e5b", 6), ("e7", 4), ("e7", 5),
        ("e5b", 7), ("e5", 7), ("e6", 6), ("e6", 7), ("e7", 6), ("e7", 7),
    ),
    (
        ("bo", 0), ("bo", 1), ("bo", 2), ("bo", 3), ("bi", 0), ("bi", 1), ("bi", 2), ("bi", 3),
        ("outer", 0), ("outer", 1), ("outer", 2), ("u1", 0), ("outer", 3), ("u1b", 0), ("u1c", 0),
        ("outer_send", 0), ("right", 0), ("u1", 1), ("u2", 0), ("l1", 0), ("u1b", 1), ("u1c", 1),
        ("u2", 1), ("u3", 0), ("u1", 2), ("l2", 0), ("u1b", 2), ("u1c", 2), ("u3", 1), ("u1", 3),
        ("u4", 0), ("u2", 2), ("l3", 0), ("u1b", 3), ("u1c", 3), ("u4", 1), ("u2", 3), ("u3", 2),
        ("l4", 0), ("u3", 3), ("u4", 2), ("u4", 3),
    ),
)


RingSum = collections.namedtuple(
    "RingSum", ("far", "near", "rest", "second", "third", "total", "sent")
)


def run(order, **stages):
    for name, k in order:
        stages[name](k)


def step_kernel(
    places, parts, order,
    grads, left, right, first, second, left_stats, right_stats,
    update_out, first_out, second_out, left_out, right_out,
    own, swap, ring, pair, cols, panel, panel_h, panel_t, panel_cat,
    basis, moment, square, turned, scaled, back_out, back, terms, terms_ring, halves, halves_out,
    outer, outer_swap, outer_ring, outer_pair, lstats, rstats, slice_t,
    load_sem, own_sem, swap_send, swap_recv, ring_send, ring_recv, pair_send, pair_recv,
    gather_send, gather_recv, panel_send, panel_recv, back_send, back_recv,
    terms_send, terms_recv, halves_send, halves_recv,
    outer_send, outer_recv, out_sem,
):
    dp = lax.axis_index("dp")
    mp = lax.axis_index("mp")
    z, yl, c = dp // 4, (dp // 2) % 2, dp % 2
    x, yh = mp // 2, mp % 2
    zn, zp, zo = (z + 1) % 4, (z + 3) % 4, (z + 2) % 4
    xn, xp, xo = (x + 1) % 4, (x + 3) % 4, (x + 2) % 4
    core_peer = {"dp": z * 4 + yl * 2 + (1 - c)}
    y_peer = {"dp": z * 4 + (1 - yl) * 2 + c}
    z_next = {"dp": zn * 4 + yl * 2 + c}
    z_prev = {"dp": zp * 4 + yl * 2 + c}
    h_peer = {"mp": x * 2 + (1 - yh)}
    q_peer = {"dp": z * 4 + (1 - yl) * 2 + c, "mp": x * 2 + (1 - yh)}
    x_next = {"mp": xn * 2 + yh}
    x_prev = {"mp": xp * 2 + yh}
    partners = (core_peer, y_peer, z_next, z_prev, h_peer, q_peer, x_next, x_prev)

    rows, width = own.shape[2], own.shape[3]
    chunks = own.shape[0]
    block = width * chunks
    half = rows // 2
    part = back.shape[2]
    hold = part * parts
    depth = panel.shape[2]

    def columns(owner, k):
        return pl.ds(pl.multiple_of(owner * block + k * width, 128), width)

    me = z * 2 + yl
    local_copy(left, panel.at[c, me], load_sem.at[0]).start()
    def piece(ref, i):
        k, lo, size = places[i]
        return ref.at[k, :, pl.ds(lo, size)]

    for i, (k, lo, size) in enumerate(places):
        for j in range(8):
            local_copy(
                grads.at[0, pl.ds(lo, size), columns(j * 2 + c, k)],
                own.at[k, j, pl.ds(lo, size)], own_sem.at[i],
            ).start()

    barrier = pltpu.get_barrier_semaphore()
    for p in partners:
        pl.semaphore_signal(barrier, inc=1, device_id=p, device_id_type=MESH)
    pl.semaphore_wait(barrier, len(partners))

    arrived(panel.at[0, 0], load_sem.at[0])

    def panel_copy(slot, n, **device):
        return remote_copy(
            panel.at[c, slot], panel.at[c, slot], panel_send.at[n], panel_recv.at[n], **device
        )

    panel_copy(me, 0, **y_peer).start()
    panel_copy(me, 1, **z_next).start()
    panel_copy(me, 2, **z_prev).start()

    for i, (k, lo, size) in enumerate(places):
        for j in range(8):
            remote_copy(
                grads.at[0, pl.ds(lo, size), columns(j * 2 + 1 - c, k)],
                swap.at[k, j, pl.ds(lo, size)],
                swap_send.at[i], swap_recv.at[i], **core_peer,
            ).start()

    local_copy(right.at[0], basis, load_sem.at[1]).start()
    local_copy(first, moment, load_sem.at[2]).start()
    local_copy(second, square, load_sem.at[3]).start()
    local_copy(left_stats, lstats, load_sem.at[4]).start()
    local_copy(right_stats.at[0], rstats, load_sem.at[5]).start()

    one = panel.at[0, 0]

    def panel_part(slot, lo, n, **device):
        piece = panel.at[c, slot, pl.ds(lo, depth // 2)]
        remote_copy(piece, piece, panel_send.at[n], panel_recv.at[n], **device).start()

    def panel_forward():
        arrived(one, panel_recv.at[1])
        panel_part(zp * 2 + yl, 0, 3, **z_next)
        panel_copy(zp * 2 + yl, 5, **y_peer).start()
        arrived(one, panel_recv.at[2])
        panel_part(zn * 2 + yl, depth // 2, 4, **z_prev)
        panel_copy(zn * 2 + yl, 6, **y_peer).start()

    def panel_forward_far():
        for n in (3, 4):
            arrived(panel.at[0, 0, pl.ds(0, depth // 2)], panel_recv.at[n])
        panel_copy(zo * 2 + yl, 17, **y_peer).start()

    def panel_share():
        for n in (0, 5, 6, 17):
            arrived(one, panel_recv.at[n])
        remote_copy(
            panel.at[c], panel.at[c], panel_send.at[7], panel_recv.at[7], **core_peer
        ).start()

    def panel_h_copy(j):
        remote_copy(
            panel.at[c, j], panel_h.at[c, j], panel_send.at[9 + j], panel_recv.at[9 + j], **q_peer
        ).start()

    def panel_turn():
        arrived(panel.at[0], panel_recv.at[7])
        for i in range(4):
            four = jnp.concatenate(
                [panel[0, 2 * i], panel[1, 2 * i], panel[0, 2 * i + 1], panel[1, 2 * i + 1]], axis=0
            )
            panel_t[:, pl.ds(i * 4 * depth, 4 * depth)] = four.T

    def panel_share_h():
        for j in range(8):
            arrived(panel.at[0, 0], panel_recv.at[9 + j])
        remote_copy(
            panel_h.at[c], panel_h.at[c], panel_send.at[8], panel_recv.at[8], **core_peer
        ).start()

    def panel_join():
        arrived(panel.at[0], panel_recv.at[8])

        def join(j, carry):
            for i in range(2):
                panel_cat[j, pl.ds(i * depth, depth)] = jnp.concatenate(
                    [panel[i, j], panel_h[i, j]], axis=1
                )
            return carry

        lax.fori_loop(0, 8, join, 0)

    def ring_stages(own, ring, send, recv, now, nxt, prv, opp, to_next, to_prev):
        def copy(j, slot, device):
            remote_copy(own.at[j], ring.at[slot], send.at[slot], recv.at[slot], **device).start()

        def far_stage(term):
            term(opp * 2)
            copy(opp * 2, 0, to_next)
            term(opp * 2 + 1)
            copy(opp * 2 + 1, 1, to_prev)

        def near_stage(term):
            term(nxt * 2 + 1)
            copy(nxt * 2 + 1, 3, to_next)
            term(prv * 2)
            copy(prv * 2, 4, to_prev)

        def rest_stage(term):
            term(nxt * 2)
            term(prv * 2 + 1)
            term(now * 2)
            term(now * 2 + 1)

        def second_stage():
            arrived(ring.at[0], recv.at[0])
            j = nxt * 2
            own[j] = (own[j].astype(F32) + ring[0].astype(F32)).astype(BF16)
            copy(j, 2, to_next)
            arrived(ring.at[1], recv.at[1])
            i = prv * 2 + 1
            own[i] = (own[i].astype(F32) + ring[1].astype(F32)).astype(BF16)
            copy(i, 5, to_prev)

        def third_stage():
            for slot in (3, 4, 2, 5):
                arrived(ring.at[slot], recv.at[slot])

        def total(which):
            return (
                own[now * 2 + which].astype(F32)
                + ring[2 + which].astype(F32)
                + ring[4 + which].astype(F32)
            )

        def sent():
            for slot in range(6):
                arrived(ring.at[slot], send.at[slot])

        return RingSum(far_stage, near_stage, rest_stage, second_stage, third_stage, total, sent)

    grad_rings = [
        ring_stages(
            piece(own, i), piece(ring, i), ring_send.at[i], ring_recv.at[i],
            z, zn, zp, zo, z_next, z_prev,
        )
        for i in range(len(places))
    ]

    def e1_term(i):
        mine, theirs = piece(own, i), piece(swap, i)

        def add(j):
            mine[j] = (mine[j].astype(F32) + theirs[j].astype(F32)).astype(BF16)

        return add

    def e1(i):
        arrived(piece(own, i), own_sem.at[i])
        arrived(piece(swap, i), swap_recv.at[i])
        grad_rings[i].far(e1_term(i))

    def e1b(i):
        grad_rings[i].near(e1_term(i))

    def e1c(i):
        grad_rings[i].rest(e1_term(i))

    def e2(i):
        grad_rings[i].second()

    def pair_piece(i):
        k, lo, size = places[i]
        return pair.at[k, pl.ds(lo, size)]

    def e3(i):
        grad_rings[i].third()
        mine = piece(own, i)
        j = z * 2 + 1 - yl
        mine[j] = grad_rings[i].total(1 - yl).astype(BF16)
        remote_copy(
            mine.at[j], pair_piece(i), pair_send.at[i], pair_recv.at[i], **y_peer
        ).start()

    def gather_piece(i, m, which=None):
        k, lo, size = places[i]
        if which is not None:
            size //= 2
            lo += which * size
        return cols.at[k, m, pl.ds(lo, size)]

    def gather_copy(i, m, n, which=None, **device):
        part = gather_piece(i, m, which)
        remote_copy(part, part, gather_send.at[i, n], gather_recv.at[i, n], **device).start()

    def gather_arrived(i, n):
        arrived(gather_piece(i, 0, None if n < 5 else 0), gather_recv.at[i, n])

    def e4(i):
        k, lo, size = places[i]
        arrived(pair_piece(i), pair_recv.at[i])
        cols[k, mp, pl.ds(lo, size)] = (
            grad_rings[i].total(yl) + pair_piece(i)[...].astype(F32)
        ).astype(BF16)
        gather_copy(i, mp, 0, **h_peer)
        gather_copy(i, mp, 1, **x_next)
        gather_copy(i, mp, 2, **x_prev)

    def e5b(i):
        gather_arrived(i, 0)
        gather_copy(i, x * 2 + 1 - yh, 3, **x_next)
        gather_copy(i, x * 2 + 1 - yh, 4, **x_prev)

    def e5(i):
        gather_arrived(i, 1)
        gather_copy(i, xp * 2 + yh, 5, 0, **x_next)
        gather_arrived(i, 2)
        gather_copy(i, xn * 2 + yh, 6, 1, **x_prev)

    def e6(i):
        gather_arrived(i, 3)
        gather_copy(i, xp * 2 + 1 - yh, 7, 0, **x_next)
        gather_arrived(i, 4)
        gather_copy(i, xn * 2 + 1 - yh, 8, 1, **x_prev)

    def e7(k):
        for i, place in enumerate(places):
            if place[0] == k:
                for n in (5, 6, 7, 8):
                    gather_arrived(i, n)
        rotated = jnp.dot(
            panel_t[...], cols[k].reshape(8 * rows, width), preferred_element_type=F32
        ).astype(BF16)
        if k == 0:
            arrived(basis, load_sem.at[1])
        for n in range(4):
            at = pl.ds(n * (block // 4), block // 4)
            term = jnp.dot(
                rotated, basis[pl.ds(k * width, width), at], preferred_element_type=F32
            )
            turned[:, at] = term if k == 0 else turned[:, at] + term

    run(
        order[0],
        e1=e1, e1b=e1b, e1c=e1c, e2=e2, e3=e3, e4=e4, e5=e5, e5b=e5b, e6=e6, e7=e7,
        panel_f1=lambda _: panel_forward(), panel_f2=lambda _: panel_forward_far(),
        panel_share=lambda _: panel_share(), panel_turn=lambda _: panel_turn(),
        panel_h=panel_h_copy, panel_share_h=lambda _: panel_share_h(),
        panel_join=lambda _: panel_join(),
    )

    arrived(moment, load_sem.at[2])
    arrived(square, load_sem.at[3])

    def moments(i, carry):
        at = pl.ds(pl.multiple_of(i * 32, 32), 32)
        t = turned[at]
        new_first = beta_first * moment[at] + (1.0 - beta_first) * t
        new_second = beta_second * square[at] + (1.0 - beta_second) * t * t
        moment[at] = new_first
        square[at] = new_second
        scaled[at] = (new_first / (jnp.sqrt(new_second) + epsilon)).astype(BF16)
        return carry

    lax.fori_loop(0, rows // 32, moments, 0)
    local_copy(moment, first_out, out_sem.at[0]).start()
    local_copy(square, second_out, out_sem.at[1]).start()

    def back_part(which, k):
        at = pl.ds(pl.multiple_of(which * hold + k * part, 128), part)
        return lax.dot_general(
            scaled[...], basis[at], (((1,), (1,)), ((), ())), preferred_element_type=F32
        ).astype(BF16)

    def back_send_part(k):
        back_out[k] = back_part(1 - yh, k)
        remote_copy(
            back_out.at[k], back.at[k, pl.ds(rows, rows)], back_send.at[k], back_recv.at[k],
            **h_peer,
        ).start()

    def back_keep_part(k):
        back[k, pl.ds(0, rows)] = back_part(yh, k)

    def outer_terms(j, carry):
        total = jnp.zeros((rows, rows), F32)
        for k in range(chunks):
            total += lax.dot_general(
                cols[k, j], cols[k, mp], (((1,), (1,)), ((), ())), preferred_element_type=F32
            )
        outer[0, j] = total[:half].astype(BF16)
        outer[1, j] = total[half:].astype(BF16)
        return carry

    def outer_part(i):
        lax.fori_loop(i * 2, i * 2 + 2, outer_terms, 0)

    def outer_share():
        remote_copy(
            outer.at[1 - c], outer_swap, outer_send.at[6], outer_recv.at[6], **core_peer
        ).start()

    outer_rings = ring_stages(
        outer.at[c], outer_ring, outer_send, outer_recv, z, zn, zp, zo, z_next, z_prev
    )

    def l1():
        arrived(outer_swap, outer_recv.at[6])

        def add(j):
            outer[c, j] = (outer[c, j].astype(F32) + outer_swap[j].astype(F32)).astype(BF16)

        outer_rings.far(add)
        outer_rings.near(add)
        outer_rings.rest(add)

    def l2():
        outer_rings.second()

    def l3():
        outer_rings.third()
        j = z * 2 + 1 - yl
        outer[c, j] = outer_rings.total(1 - yl).astype(BF16)
        remote_copy(
            outer.at[c, j], outer_pair, outer_send.at[7], outer_recv.at[7], **y_peer
        ).start()

    def l4():
        arrived(outer_pair, outer_recv.at[7])
        arrived(lstats, load_sem.at[4])
        total = outer_rings.total(yl) + outer_pair[...].astype(F32)
        lstats[...] = beta_stats * lstats[...] + (1.0 - beta_stats) * total
        local_copy(lstats, left_out, out_sem.at[2]).start()

    def right_terms():
        share = rstats.shape[0]
        k_own = (mp * share) // width
        off = pl.ds(pl.multiple_of((mp * share) % width, 128), share)
        for i in range(4):
            two = cols[k_own, pl.ds(2 * i, 2), :, off].reshape(2 * rows, share)
            slice_t[:, pl.ds(i * 2 * rows, 2 * rows)] = two.T
        arrived(rstats, load_sem.at[5])
        for k in range(chunks):
            at = pl.ds(k * width, width)
            term = jnp.dot(
                slice_t[...], cols[k].reshape(8 * rows, width), preferred_element_type=F32
            )
            rstats[:, at] = beta_stats * rstats[:, at] + (1.0 - beta_stats) * term
        local_copy(rstats, right_out.at[0], out_sem.at[3]).start()

    term_rings = [
        ring_stages(
            terms.at[k], terms_ring.at[k], terms_send.at[k], terms_recv.at[k],
            x, xn, xp, xo, x_next, x_prev,
        )
        for k in range(parts)
    ]

    def u1_term(k):
        def term(j):
            terms[k, j] = jnp.dot(
                panel_cat[j], back[k], preferred_element_type=F32
            ).astype(BF16)

        return term

    def u1(k):
        arrived(back.at[k, pl.ds(0, rows)], back_recv.at[k])
        term_rings[k].far(u1_term(k))

    def u1b(k):
        term_rings[k].near(u1_term(k))

    def u1c(k):
        term_rings[k].rest(u1_term(k))

    def u2(k):
        term_rings[k].second()

    def u3(k):
        term_rings[k].third()
        halves_out[k] = term_rings[k].total(1 - yh).astype(BF16)
        remote_copy(
            halves_out.at[k], halves.at[yh, k], halves_send.at[k], halves_recv.at[k], **h_peer
        ).start()
        halves[yh, k] = term_rings[k].total(yh).astype(BF16)
        local_copy(
            halves.at[yh, k],
            update_out.at[:, pl.ds(pl.multiple_of(yh * hold + k * part, 128), part)],
            out_sem.at[4],
        ).start()

    def u4(k):
        arrived(halves.at[0, k], halves_recv.at[k])
        local_copy(
            halves.at[1 - yh, k],
            update_out.at[:, pl.ds(pl.multiple_of((1 - yh) * hold + k * part, 128), part)],
            out_sem.at[5],
        ).start()

    run(
        order[1],
        bo=back_send_part, bi=back_keep_part, u1=u1, u1b=u1b, u1c=u1c, u2=u2, u3=u3, u4=u4,
        outer=outer_part, outer_send=lambda _: outer_share(),
        l1=lambda _: l1(), l2=lambda _: l2(), l3=lambda _: l3(), l4=lambda _: l4(),
        right=lambda _: right_terms(),
    )

    for n in (0, 1, 2, 5, 6, 17):
        arrived(panel.at[0, 0], panel_send.at[n])
    for n in (3, 4):
        arrived(panel.at[0, 0, pl.ds(0, depth // 2)], panel_send.at[n])
    for n in range(7, 9):
        arrived(panel.at[0], panel_send.at[n])
    for n in range(9, 17):
        arrived(panel.at[0, 0], panel_send.at[n])
    for i in range(len(places)):
        arrived(piece(swap, i), swap_send.at[i])
        grad_rings[i].sent()
        arrived(pair_piece(i), pair_send.at[i])
        for n in range(9):
            arrived(gather_piece(i, 0, None if n < 5 else 0), gather_send.at[i, n])
    for k in range(parts):
        arrived(back_out.at[k], back_send.at[k])
        term_rings[k].sent()
        arrived(halves_out.at[k], halves_send.at[k])
    outer_rings.sent()
    arrived(outer_swap, outer_send.at[6])
    arrived(outer_pair, outer_send.at[7])
    arrived(moment, out_sem.at[0])
    arrived(square, out_sem.at[1])
    arrived(lstats, out_sem.at[2])
    arrived(rstats, out_sem.at[3])
    arrived(halves.at[0], out_sem.at[4])
    arrived(halves.at[0], out_sem.at[5])


def hand_over(*refs):
    ins, outs, buffers, in_sems, out_sems = refs[:5], refs[5:10], refs[10:15], refs[15], refs[16]
    cuts = 4
    pieces = []
    for i in range(5):
        count = cuts if i < 3 else 1
        size = ins[i].shape[0] // count
        for n in range(count):
            at = pl.ds(n * size, size)
            pieces.append((i, n, at))
    for i, n, at in pieces:
        local_copy(ins[i].at[at], buffers[i].at[at], in_sems.at[i, n]).start()
    for i, n, at in pieces:
        arrived(buffers[i].at[at], in_sems.at[i, n])
        local_copy(buffers[i].at[at], outs[i].at[at], out_sems.at[i, n]).start()
    for i, n, at in pieces:
        arrived(buffers[i].at[at], out_sems.at[i, n])


def on_device(
    gradients, left_basis, right_basis, first_moment, second_moment, left_stats, right_stats,
    chunks=8, parts=4, places=PLACES, order=ORDER,
):
    rows, block = gradients.shape[1], gradients.shape[2] // 16
    width = block // chunks
    part = block // 2 // parts
    depth, span = left_basis.shape
    share = right_stats.shape[1]
    dma = pltpu.SemaphoreType.DMA
    any_space = pl.BlockSpec(memory_space=pl.ANY)

    def buffer(*shape, dtype=BF16):
        return pltpu.VMEM(shape, dtype)

    results = pl.pallas_call(
        functools.partial(step_kernel, places, parts, order),
        name="soap_step",
        out_shape=(
            jax.ShapeDtypeStruct((rows, block), BF16),
            jax.ShapeDtypeStruct((rows, block), F32),
            jax.ShapeDtypeStruct((rows, block), F32),
            jax.ShapeDtypeStruct((depth, span), F32),
            jax.ShapeDtypeStruct((1, share, block), F32),
        ),
        in_specs=[any_space] * 7,
        out_specs=(any_space,) * 5,
        scratch_shapes=[
            buffer(chunks, 8, rows, width),
            buffer(chunks, 8, rows, width),
            buffer(chunks, 6, rows, width),
            buffer(chunks, rows, width),
            buffer(chunks, 8, rows, width),
            buffer(2, 8, depth, span),
            buffer(2, 8, depth, span),
            buffer(span, 16 * depth),
            buffer(8, 2 * depth, 2 * span),
            buffer(block, block),
            buffer(rows, block, dtype=F32),
            buffer(rows, block, dtype=F32),
            buffer(rows, block, dtype=F32),
            buffer(rows, block),
            buffer(parts, rows, part),
            buffer(parts, 2 * rows, part),
            buffer(parts, 8, rows, part),
            buffer(parts, 6, rows, part),
            buffer(2, parts, rows, part),
            buffer(parts, rows, part),
            buffer(2, 8, depth, span),
            buffer(8, depth, span),
            buffer(6, depth, span),
            buffer(depth, span),
            buffer(depth, span, dtype=F32),
            buffer(share, block, dtype=F32),
            buffer(share, 8 * rows),
            dma((6,)),
            dma((len(places),)),
            dma((len(places),)),
            dma((len(places),)),
            dma((len(places), 6)),
            dma((len(places), 6)),
            dma((len(places),)),
            dma((len(places),)),
            dma((len(places), 9)),
            dma((len(places), 9)),
            dma((18,)),
            dma((18,)),
            dma((parts,)),
            dma((parts,)),
            dma((parts, 6)),
            dma((parts, 6)),
            dma((parts,)),
            dma((parts,)),
            dma((8,)),
            dma((8,)),
            dma((6,)),
        ],
        compiler_params=pltpu.CompilerParams(
            collective_id=0, has_side_effects=True, vmem_limit_bytes=62 * 1024 * 1024
        ),
    )(gradients, left_basis, right_basis, first_moment, second_moment, left_stats, right_stats)
    return pl.pallas_call(
        hand_over,
        name="hand_over",
        out_shape=tuple(jax.ShapeDtypeStruct(r.shape, r.dtype) for r in results),
        in_specs=[any_space] * 5,
        out_specs=(any_space,) * 5,
        scratch_shapes=[pltpu.VMEM(r.shape, r.dtype) for r in results] + [dma((5, 4)), dma((5, 4))],
    )(*results)


def solution(mesh):
    return jax.shard_map(
        on_device,
        mesh=mesh,
        in_specs=(
            P("dp", "mp", None),
            P("dp", "mp"),
            P("dp", None, None),
            P("mp", "dp"),
            P("mp", "dp"),
            P("dp", "mp"),
            P("dp", "mp", None),
        ),
        out_specs=(P("mp", "dp"), P("mp", "dp"), P("mp", "dp"), P("dp", "mp"), P("dp", "mp", None)),
        check_vma=False,
    )
```

```python
import collections
import functools

import jax
import jax.numpy as jnp
from jax import lax
from jax.experimental import pallas as pl
from jax.experimental.pallas import tpu as pltpu
from jax.sharding import PartitionSpec as P

MESH = pl.DeviceIdType.MESH
beta_first = 0.9
beta_second = 0.95
beta_stats = 0.95
epsilon = 1e-08

F32 = jnp.float32
BF16 = jnp.bfloat16


def local_copy(src, dst, sem):
    return pltpu.make_async_copy(src, dst, sem)


def remote_copy(src, dst, send, recv, **device):
    return pltpu.make_async_remote_copy(
        src_ref=src,
        dst_ref=dst,
        send_sem=send,
        recv_sem=recv,
        device_id=device,
        device_id_type=MESH,
    )


def arrived(ref, sem):
    pltpu.make_async_copy(ref, ref, sem).wait()


PLACES = (
    (0, 0, 320), (1, 0, 320), (2, 0, 320), (3, 0, 320), (4, 0, 320), (5, 0, 320),
    (6, 0, 320), (7, 0, 320),
)

ORDER = (
    (
        ("e1", 0), ("e1b", 0), ("e1c", 0), ("panel_f1", 0), ("e1", 1), ("e2", 0), ("panel_f2", 0),
        ("e1b", 1), ("e1c", 1), ("e2", 1), ("e3", 0), ("e1", 2), ("panel_share", 0),
        ("panel_h", 0), ("e1b", 2), ("e1c", 2), ("e3", 1), ("e1", 3), ("e4", 0),
        ("panel_turn", 0), ("e2", 2), ("panel_h", 1), ("e1b", 3), ("e1c", 3), ("e4", 1),
        ("e5", 0), ("e2", 3), ("e5b", 0), ("e3", 2), ("e1", 4), ("panel_h", 2), ("e5", 1),
        ("e1b", 4), ("e1c", 4), ("e5b", 1), ("panel_h", 3), ("e3", 3), ("e1", 5), ("e4", 2),
        ("e6", 0), ("e2", 4), ("e6", 1), ("e1b", 5), ("e1c", 5), ("panel_h", 4), ("e4", 3),
        ("e5", 2), ("e2", 5), ("e7", 0), ("e5b", 2), ("e3", 4), ("e1", 6), ("e7", 1),
        ("panel_h", 5), ("e5", 3), ("e1b", 6), ("e1c", 6), ("e3", 5), ("e1", 7), ("e5b", 3),
        ("panel_h", 6), ("e6", 2), ("e4", 4), ("e2", 6), ("e1b", 7), ("e1c", 7), ("e4", 5),
        ("e6", 3), ("e2", 7), ("e7", 2), ("e3", 6), ("panel_h", 7), ("e5", 4), ("e5b", 4),
        ("e5", 5), ("e5b", 5), ("e7", 3), ("e3", 7), ("e4", 6), ("panel_share_h", 0), ("e6", 4),
        ("e6", 5), ("e4", 7), ("panel_join", 0), ("e5", 6), ("e5b", 6), ("e7", 4), ("e7", 5),
        ("e5b", 7), ("e5", 7), ("e6", 6), ("e6", 7), ("e7", 6), ("e7", 7),
    ),
    (
        ("bo", 0), ("bo", 1), ("bo", 2), ("bo", 3), ("bi", 0), ("bi", 1), ("bi", 2), ("bi", 3),
        ("outer", 0), ("outer", 1), ("outer", 2), ("outer", 3), ("outer", 4), ("u1", 0),
        ("outer", 5), ("u1b", 0), ("u1c", 0), ("outer", 6), ("u1", 1), ("outer", 7),
        ("outer_send", 0), ("right", 0), ("right", 1), ("u1b", 1), ("u1c", 1), ("u2", 0),
        ("right", 2), ("right", 3), ("right", 4), ("right", 5), ("right", 6), ("right", 7),
        ("l1", 0), ("u1", 2), ("u2", 1), ("u1b", 2), ("u1c", 2), ("u3", 0), ("l2", 0), ("u1", 3),
        ("u2", 2), ("u3", 1), ("u4", 0), ("u1b", 3), ("u1c", 3), ("l3", 0), ("u2", 3), ("u4", 1),
        ("u3", 2), ("l4", 0), ("u3", 3), ("u4", 2), ("u4", 3),
    ),
)


RingSum = collections.namedtuple(
    "RingSum", ("far", "near", "rest", "second", "third", "total", "sent")
)


def run(order, **stages):
    for name, k in order:
        stages[name](k)


def step_kernel(
    places, parts, order,
    grads, left, right, first, second, left_stats, right_stats,
    update_out, first_out, second_out, left_out, right_out,
    own, swap, ring, pair, cols, panel, panel_h, panel_t, panel_cat,
    basis, moment, square, turned, scaled, back_out, back, terms, terms_ring, halves, halves_out,
    outer, outer_swap, outer_ring, outer_pair, lstats, rstats, slice_t,
    load_sem, own_sem, swap_send, swap_recv, ring_send, ring_recv, pair_send, pair_recv,
    gather_send, gather_recv, panel_send, panel_recv, back_send, back_recv,
    terms_send, terms_recv, halves_send, halves_recv,
    outer_send, outer_recv, out_sem,
):
    dp = lax.axis_index("dp")
    mp = lax.axis_index("mp")
    z, yl, c = dp // 4, (dp // 2) % 2, dp % 2
    x, yh = mp // 2, mp % 2
    zn, zp, zo = (z + 1) % 4, (z + 3) % 4, (z + 2) % 4
    xn, xp, xo = (x + 1) % 4, (x + 3) % 4, (x + 2) % 4
    core_peer = {"dp": z * 4 + yl * 2 + (1 - c)}
    y_peer = {"dp": z * 4 + (1 - yl) * 2 + c}
    z_next = {"dp": zn * 4 + yl * 2 + c}
    z_prev = {"dp": zp * 4 + yl * 2 + c}
    h_peer = {"mp": x * 2 + (1 - yh)}
    q_peer = {"dp": z * 4 + (1 - yl) * 2 + c, "mp": x * 2 + (1 - yh)}
    x_next = {"mp": xn * 2 + yh}
    x_prev = {"mp": xp * 2 + yh}
    partners = (core_peer, y_peer, z_next, z_prev, h_peer, q_peer, x_next, x_prev)

    rows, width = own.shape[2], own.shape[3]
    chunks = own.shape[0]
    block = width * chunks
    half = rows // 2
    part = back.shape[2]
    hold = part * parts
    depth = panel.shape[2]

    def columns(owner, k):
        return pl.ds(pl.multiple_of(owner * block + k * width, 128), width)

    me = z * 2 + yl
    local_copy(left, panel.at[c, me], load_sem.at[0]).start()
    def piece(ref, i):
        k, lo, size = places[i]
        return ref.at[k, :, pl.ds(lo, size)]

    for i, (k, lo, size) in enumerate(places):
        for j in range(8):
            local_copy(
                grads.at[0, pl.ds(lo, size), columns(j * 2 + c, k)],
                own.at[k, j, pl.ds(lo, size)], own_sem.at[i],
            ).start()

    barrier = pltpu.get_barrier_semaphore()
    for p in partners:
        pl.semaphore_signal(barrier, inc=1, device_id=p, device_id_type=MESH)
    pl.semaphore_wait(barrier, len(partners))

    arrived(panel.at[0, 0], load_sem.at[0])

    def panel_copy(slot, n, **device):
        return remote_copy(
            panel.at[c, slot], panel.at[c, slot], panel_send.at[n], panel_recv.at[n], **device
        )

    panel_copy(me, 0, **y_peer).start()
    panel_copy(me, 1, **z_next).start()
    panel_copy(me, 2, **z_prev).start()

    for i, (k, lo, size) in enumerate(places):
        for j in range(8):
            remote_copy(
                grads.at[0, pl.ds(lo, size), columns(j * 2 + 1 - c, k)],
                swap.at[k, j, pl.ds(lo, size)],
                swap_send.at[i], swap_recv.at[i], **core_peer,
            ).start()

    local_copy(right.at[0], basis, load_sem.at[1]).start()
    local_copy(first, moment, load_sem.at[2]).start()
    local_copy(second, square, load_sem.at[3]).start()
    local_copy(left_stats, lstats, load_sem.at[4]).start()
    local_copy(right_stats.at[0], rstats, load_sem.at[5]).start()

    one = panel.at[0, 0]

    def panel_part(slot, lo, n, **device):
        piece = panel.at[c, slot, pl.ds(lo, depth // 2)]
        remote_copy(piece, piece, panel_send.at[n], panel_recv.at[n], **device).start()

    def panel_forward():
        arrived(one, panel_recv.at[1])
        panel_part(zp * 2 + yl, 0, 3, **z_next)
        panel_copy(zp * 2 + yl, 5, **y_peer).start()
        arrived(one, panel_recv.at[2])
        panel_part(zn * 2 + yl, depth // 2, 4, **z_prev)
        panel_copy(zn * 2 + yl, 6, **y_peer).start()

    def panel_forward_far():
        for n in (3, 4):
            arrived(panel.at[0, 0, pl.ds(0, depth // 2)], panel_recv.at[n])
        panel_copy(zo * 2 + yl, 17, **y_peer).start()

    def panel_share():
        for n in (0, 5, 6, 17):
            arrived(one, panel_recv.at[n])
        remote_copy(
            panel.at[c], panel.at[c], panel_send.at[7], panel_recv.at[7], **core_peer
        ).start()

    def panel_h_copy(j):
        remote_copy(
            panel.at[c, j], panel_h.at[c, j], panel_send.at[9 + j], panel_recv.at[9 + j], **q_peer
        ).start()

    def panel_turn():
        arrived(panel.at[0], panel_recv.at[7])
        for i in range(4):
            four = jnp.concatenate(
                [panel[0, 2 * i], panel[1, 2 * i], panel[0, 2 * i + 1], panel[1, 2 * i + 1]], axis=0
            )
            panel_t[:, pl.ds(i * 4 * depth, 4 * depth)] = four.T

    def panel_share_h():
        for j in range(8):
            arrived(panel.at[0, 0], panel_recv.at[9 + j])
        remote_copy(
            panel_h.at[c], panel_h.at[c], panel_send.at[8], panel_recv.at[8], **core_peer
        ).start()

    def panel_join():
        arrived(panel.at[0], panel_recv.at[8])

        def join(j, carry):
            for i in range(2):
                panel_cat[j, pl.ds(i * depth, depth)] = jnp.concatenate(
                    [panel[i, j], panel_h[i, j]], axis=1
                )
            return carry

        lax.fori_loop(0, 8, join, 0)

    def ring_stages(own, ring, send, recv, now, nxt, prv, opp, to_next, to_prev):
        def copy(j, slot, device):
            remote_copy(own.at[j], ring.at[slot], send.at[slot], recv.at[slot], **device).start()

        def far_stage(term):
            term(opp * 2)
            copy(opp * 2, 0, to_next)
            term(opp * 2 + 1)
            copy(opp * 2 + 1, 1, to_prev)

        def near_stage(term):
            term(nxt * 2 + 1)
            copy(nxt * 2 + 1, 3, to_next)
            term(prv * 2)
            copy(prv * 2, 4, to_prev)

        def rest_stage(term):
            term(nxt * 2)
            term(prv * 2 + 1)
            term(now * 2)
            term(now * 2 + 1)

        def second_stage():
            arrived(ring.at[0], recv.at[0])
            j = nxt * 2
            own[j] = (own[j].astype(F32) + ring[0].astype(F32)).astype(BF16)
            copy(j, 2, to_next)
            arrived(ring.at[1], recv.at[1])
            i = prv * 2 + 1
            own[i] = (own[i].astype(F32) + ring[1].astype(F32)).astype(BF16)
            copy(i, 5, to_prev)

        def third_stage():
            for slot in (3, 4, 2, 5):
                arrived(ring.at[slot], recv.at[slot])

        def total(which):
            return (
                own[now * 2 + which].astype(F32)
                + ring[2 + which].astype(F32)
                + ring[4 + which].astype(F32)
            )

        def sent():
            for slot in range(6):
                arrived(ring.at[slot], send.at[slot])

        return RingSum(far_stage, near_stage, rest_stage, second_stage, third_stage, total, sent)

    grad_rings = [
        ring_stages(
            piece(own, i), piece(ring, i), ring_send.at[i], ring_recv.at[i],
            z, zn, zp, zo, z_next, z_prev,
        )
        for i in range(len(places))
    ]

    def e1_term(i):
        mine, theirs = piece(own, i), piece(swap, i)

        def add(j):
            mine[j] = (mine[j].astype(F32) + theirs[j].astype(F32)).astype(BF16)

        return add

    def e1(i):
        arrived(piece(own, i), own_sem.at[i])
        arrived(piece(swap, i), swap_recv.at[i])
        grad_rings[i].far(e1_term(i))

    def e1b(i):
        grad_rings[i].near(e1_term(i))

    def e1c(i):
        grad_rings[i].rest(e1_term(i))

    def e2(i):
        grad_rings[i].second()

    def pair_piece(i):
        k, lo, size = places[i]
        return pair.at[k, pl.ds(lo, size)]

    def e3(i):
        grad_rings[i].third()
        mine = piece(own, i)
        j = z * 2 + 1 - yl
        mine[j] = grad_rings[i].total(1 - yl).astype(BF16)
        remote_copy(
            mine.at[j], pair_piece(i), pair_send.at[i], pair_recv.at[i], **y_peer
        ).start()

    def gather_piece(i, m, which=None):
        k, lo, size = places[i]
        if which is not None:
            size //= 2
            lo += which * size
        return cols.at[k, m, pl.ds(lo, size)]

    def gather_copy(i, m, n, which=None, **device):
        part = gather_piece(i, m, which)
        remote_copy(part, part, gather_send.at[i, n], gather_recv.at[i, n], **device).start()

    def gather_arrived(i, n):
        arrived(gather_piece(i, 0, None if n < 5 else 0), gather_recv.at[i, n])

    def e4(i):
        k, lo, size = places[i]
        arrived(pair_piece(i), pair_recv.at[i])
        cols[k, mp, pl.ds(lo, size)] = (
            grad_rings[i].total(yl) + pair_piece(i)[...].astype(F32)
        ).astype(BF16)
        gather_copy(i, mp, 0, **h_peer)
        gather_copy(i, mp, 1, **x_next)
        gather_copy(i, mp, 2, **x_prev)

    def e5b(i):
        gather_arrived(i, 0)
        gather_copy(i, x * 2 + 1 - yh, 3, **x_next)
        gather_copy(i, x * 2 + 1 - yh, 4, **x_prev)

    def e5(i):
        gather_arrived(i, 1)
        gather_copy(i, xp * 2 + yh, 5, 0, **x_next)
        gather_arrived(i, 2)
        gather_copy(i, xn * 2 + yh, 6, 1, **x_prev)

    def e6(i):
        gather_arrived(i, 3)
        gather_copy(i, xp * 2 + 1 - yh, 7, 0, **x_next)
        gather_arrived(i, 4)
        gather_copy(i, xn * 2 + 1 - yh, 8, 1, **x_prev)

    def e7(k):
        for i, place in enumerate(places):
            if place[0] == k:
                for n in (5, 6, 7, 8):
                    gather_arrived(i, n)
        rotated = jnp.dot(
            panel_t[...], cols[k].reshape(8 * rows, width), preferred_element_type=F32
        ).astype(BF16)
        if k == 0:
            arrived(basis, load_sem.at[1])
        for n in range(4):
            at = pl.ds(n * (block // 4), block // 4)
            term = jnp.dot(
                rotated, basis[pl.ds(k * width, width), at], preferred_element_type=F32
            )
            turned[:, at] = term if k == 0 else turned[:, at] + term

    run(
        order[0],
        e1=e1, e1b=e1b, e1c=e1c, e2=e2, e3=e3, e4=e4, e5=e5, e5b=e5b, e6=e6, e7=e7,
        panel_f1=lambda _: panel_forward(), panel_f2=lambda _: panel_forward_far(),
        panel_share=lambda _: panel_share(), panel_turn=lambda _: panel_turn(),
        panel_h=panel_h_copy, panel_share_h=lambda _: panel_share_h(),
        panel_join=lambda _: panel_join(),
    )

    arrived(moment, load_sem.at[2])
    arrived(square, load_sem.at[3])

    def moments(i, carry):
        at = pl.ds(pl.multiple_of(i * 32, 32), 32)
        t = turned[at]
        new_first = beta_first * moment[at] + (1.0 - beta_first) * t
        new_second = beta_second * square[at] + (1.0 - beta_second) * t * t
        moment[at] = new_first
        square[at] = new_second
        scaled[at] = (new_first / (jnp.sqrt(new_second) + epsilon)).astype(BF16)
        return carry

    lax.fori_loop(0, rows // 32, moments, 0)
    local_copy(moment, first_out, out_sem.at[0]).start()
    local_copy(square, second_out, out_sem.at[1]).start()

    def back_part(which, k):
        at = pl.ds(pl.multiple_of(which * hold + k * part, 128), part)
        return lax.dot_general(
            scaled[...], basis[at], (((1,), (1,)), ((), ())), preferred_element_type=F32
        ).astype(BF16)

    def back_send_part(k):
        back_out[k] = back_part(1 - yh, k)
        remote_copy(
            back_out.at[k], back.at[k, pl.ds(rows, rows)], back_send.at[k], back_recv.at[k],
            **h_peer,
        ).start()

    def back_keep_part(k):
        back[k, pl.ds(0, rows)] = back_part(yh, k)

    def outer_terms(j, carry):
        total = jnp.zeros((rows, rows), F32)
        for k in range(chunks):
            total += lax.dot_general(
                cols[k, j], cols[k, mp], (((1,), (1,)), ((), ())), preferred_element_type=F32
            )
        outer[0, j] = total[:half].astype(BF16)
        outer[1, j] = total[half:].astype(BF16)
        return carry

    def outer_part(i):
        lax.fori_loop(i, i + 1, outer_terms, 0)

    def outer_share():
        remote_copy(
            outer.at[1 - c], outer_swap, outer_send.at[6], outer_recv.at[6], **core_peer
        ).start()

    outer_rings = ring_stages(
        outer.at[c], outer_ring, outer_send, outer_recv, z, zn, zp, zo, z_next, z_prev
    )

    def l1():
        arrived(outer_swap, outer_recv.at[6])

        def add(j):
            outer[c, j] = (outer[c, j].astype(F32) + outer_swap[j].astype(F32)).astype(BF16)

        outer_rings.far(add)
        outer_rings.near(add)
        outer_rings.rest(add)

    def l2():
        outer_rings.second()

    def l3():
        outer_rings.third()
        j = z * 2 + 1 - yl
        outer[c, j] = outer_rings.total(1 - yl).astype(BF16)
        remote_copy(
            outer.at[c, j], outer_pair, outer_send.at[7], outer_recv.at[7], **y_peer
        ).start()

    def l4():
        arrived(outer_pair, outer_recv.at[7])
        arrived(lstats, load_sem.at[4])
        total = outer_rings.total(yl) + outer_pair[...].astype(F32)
        lstats[...] = beta_stats * lstats[...] + (1.0 - beta_stats) * total
        local_copy(lstats, left_out, out_sem.at[2]).start()

    def right_terms(k):
        if k == 0:
            share = rstats.shape[0]
            k_own = (mp * share) // width
            off = pl.ds(pl.multiple_of((mp * share) % width, 128), share)
            for i in range(4):
                two = cols[k_own, pl.ds(2 * i, 2), :, off].reshape(2 * rows, share)
                slice_t[:, pl.ds(i * 2 * rows, 2 * rows)] = two.T
            arrived(rstats, load_sem.at[5])
        at = pl.ds(k * width, width)
        term = jnp.dot(slice_t[...], cols[k].reshape(8 * rows, width), preferred_element_type=F32)
        rstats[:, at] = beta_stats * rstats[:, at] + (1.0 - beta_stats) * term
        if k == chunks - 1:
            local_copy(rstats, right_out.at[0], out_sem.at[3]).start()

    term_rings = [
        ring_stages(
            terms.at[k], terms_ring.at[k], terms_send.at[k], terms_recv.at[k],
            x, xn, xp, xo, x_next, x_prev,
        )
        for k in range(parts)
    ]

    def u1_term(k):
        def term(j):
            terms[k, j] = jnp.dot(
                panel_cat[j], back[k], preferred_element_type=F32
            ).astype(BF16)

        return term

    def u1(k):
        arrived(back.at[k, pl.ds(0, rows)], back_recv.at[k])
        term_rings[k].far(u1_term(k))

    def u1b(k):
        term_rings[k].near(u1_term(k))

    def u1c(k):
        term_rings[k].rest(u1_term(k))

    def u2(k):
        term_rings[k].second()

    def u3(k):
        term_rings[k].third()
        halves_out[k] = term_rings[k].total(1 - yh).astype(BF16)
        remote_copy(
            halves_out.at[k], halves.at[yh, k], halves_send.at[k], halves_recv.at[k], **h_peer
        ).start()
        halves[yh, k] = term_rings[k].total(yh).astype(BF16)
        local_copy(
            halves.at[yh, k],
            update_out.at[:, pl.ds(pl.multiple_of(yh * hold + k * part, 128), part)],
            out_sem.at[4],
        ).start()

    def u4(k):
        arrived(halves.at[0, k], halves_recv.at[k])
        local_copy(
            halves.at[1 - yh, k],
            update_out.at[:, pl.ds(pl.multiple_of((1 - yh) * hold + k * part, 128), part)],
            out_sem.at[5],
        ).start()

    run(
        order[1],
        bo=back_send_part, bi=back_keep_part, u1=u1, u1b=u1b, u1c=u1c, u2=u2, u3=u3, u4=u4,
        outer=outer_part, outer_send=lambda _: outer_share(),
        l1=lambda _: l1(), l2=lambda _: l2(), l3=lambda _: l3(), l4=lambda _: l4(),
        right=right_terms,
    )

    for n in (0, 1, 2, 5, 6, 17):
        arrived(panel.at[0, 0], panel_send.at[n])
    for n in (3, 4):
        arrived(panel.at[0, 0, pl.ds(0, depth // 2)], panel_send.at[n])
    for n in range(7, 9):
        arrived(panel.at[0], panel_send.at[n])
    for n in range(9, 17):
        arrived(panel.at[0, 0], panel_send.at[n])
    for i in range(len(places)):
        arrived(piece(swap, i), swap_send.at[i])
        grad_rings[i].sent()
        arrived(pair_piece(i), pair_send.at[i])
        for n in range(9):
            arrived(gather_piece(i, 0, None if n < 5 else 0), gather_send.at[i, n])
    for k in range(parts):
        arrived(back_out.at[k], back_send.at[k])
        term_rings[k].sent()
        arrived(halves_out.at[k], halves_send.at[k])
    outer_rings.sent()
    arrived(outer_swap, outer_send.at[6])
    arrived(outer_pair, outer_send.at[7])
    arrived(moment, out_sem.at[0])
    arrived(square, out_sem.at[1])
    arrived(lstats, out_sem.at[2])
    arrived(rstats, out_sem.at[3])
    arrived(halves.at[0], out_sem.at[4])
    arrived(halves.at[0], out_sem.at[5])


def hand_over(*refs):
    ins, outs, buffers, in_sems, out_sems = refs[:5], refs[5:10], refs[10:15], refs[15], refs[16]
    cuts = 4
    pieces = []
    for i in range(5):
        count = cuts if i < 3 else 1
        size = ins[i].shape[0] // count
        for n in range(count):
            at = pl.ds(n * size, size)
            pieces.append((i, n, at))
    for i, n, at in pieces:
        local_copy(ins[i].at[at], buffers[i].at[at], in_sems.at[i, n]).start()
    for i, n, at in pieces:
        arrived(buffers[i].at[at], in_sems.at[i, n])
        local_copy(buffers[i].at[at], outs[i].at[at], out_sems.at[i, n]).start()
    for i, n, at in pieces:
        arrived(buffers[i].at[at], out_sems.at[i, n])


def on_device(
    gradients, left_basis, right_basis, first_moment, second_moment, left_stats, right_stats,
    chunks=8, parts=4, places=PLACES, order=ORDER,
):
    rows, block = gradients.shape[1], gradients.shape[2] // 16
    width = block // chunks
    part = block // 2 // parts
    depth, span = left_basis.shape
    share = right_stats.shape[1]
    dma = pltpu.SemaphoreType.DMA
    any_space = pl.BlockSpec(memory_space=pl.ANY)

    def buffer(*shape, dtype=BF16):
        return pltpu.VMEM(shape, dtype)

    results = pl.pallas_call(
        functools.partial(step_kernel, places, parts, order),
        name="soap_step",
        out_shape=(
            jax.ShapeDtypeStruct((rows, block), BF16),
            jax.ShapeDtypeStruct((rows, block), F32),
            jax.ShapeDtypeStruct((rows, block), F32),
            jax.ShapeDtypeStruct((depth, span), F32),
            jax.ShapeDtypeStruct((1, share, block), F32),
        ),
        in_specs=[any_space] * 7,
        out_specs=(any_space,) * 5,
        scratch_shapes=[
            buffer(chunks, 8, rows, width),
            buffer(chunks, 8, rows, width),
            buffer(chunks, 6, rows, width),
            buffer(chunks, rows, width),
            buffer(chunks, 8, rows, width),
            buffer(2, 8, depth, span),
            buffer(2, 8, depth, span),
            buffer(span, 16 * depth),
            buffer(8, 2 * depth, 2 * span),
            buffer(block, block),
            buffer(rows, block, dtype=F32),
            buffer(rows, block, dtype=F32),
            buffer(rows, block, dtype=F32),
            buffer(rows, block),
            buffer(parts, rows, part),
            buffer(parts, 2 * rows, part),
            buffer(parts, 8, rows, part),
            buffer(parts, 6, rows, part),
            buffer(2, parts, rows, part),
            buffer(parts, rows, part),
            buffer(2, 8, depth, span),
            buffer(8, depth, span),
            buffer(6, depth, span),
            buffer(depth, span),
            buffer(depth, span, dtype=F32),
            buffer(share, block, dtype=F32),
            buffer(share, 8 * rows),
            dma((6,)),
            dma((len(places),)),
            dma((len(places),)),
            dma((len(places),)),
            dma((len(places), 6)),
            dma((len(places), 6)),
            dma((len(places),)),
            dma((len(places),)),
            dma((len(places), 9)),
            dma((len(places), 9)),
            dma((18,)),
            dma((18,)),
            dma((parts,)),
            dma((parts,)),
            dma((parts, 6)),
            dma((parts, 6)),
            dma((parts,)),
            dma((parts,)),
            dma((8,)),
            dma((8,)),
            dma((6,)),
        ],
        compiler_params=pltpu.CompilerParams(
            collective_id=0, has_side_effects=True, vmem_limit_bytes=62 * 1024 * 1024
        ),
    )(gradients, left_basis, right_basis, first_moment, second_moment, left_stats, right_stats)
    return pl.pallas_call(
        hand_over,
        name="hand_over",
        out_shape=tuple(jax.ShapeDtypeStruct(r.shape, r.dtype) for r in results),
        in_specs=[any_space] * 5,
        out_specs=(any_space,) * 5,
        scratch_shapes=[pltpu.VMEM(r.shape, r.dtype) for r in results] + [dma((5, 4)), dma((5, 4))],
    )(*results)


def solution(mesh):
    return jax.shard_map(
        on_device,
        mesh=mesh,
        in_specs=(
            P("dp", "mp", None),
            P("dp", "mp"),
            P("dp", None, None),
            P("mp", "dp"),
            P("mp", "dp"),
            P("dp", "mp"),
            P("dp", "mp", None),
        ),
        out_specs=(P("mp", "dp"), P("mp", "dp"), P("mp", "dp"), P("dp", "mp"), P("dp", "mp", None)),
        check_vma=False,
    )
```

```python
import collections
import functools

import jax
import jax.numpy as jnp
from jax import lax
from jax.experimental import pallas as pl
from jax.experimental.pallas import tpu as pltpu
from jax.sharding import PartitionSpec as P

MESH = pl.DeviceIdType.MESH
beta_first = 0.9
beta_second = 0.95
beta_stats = 0.95
epsilon = 1e-08

F32 = jnp.float32
BF16 = jnp.bfloat16


def local_copy(src, dst, sem):
    return pltpu.make_async_copy(src, dst, sem)


def remote_copy(src, dst, send, recv, **device):
    return pltpu.make_async_remote_copy(
        src_ref=src,
        dst_ref=dst,
        send_sem=send,
        recv_sem=recv,
        device_id=device,
        device_id_type=MESH,
    )


def arrived(ref, sem):
    pltpu.make_async_copy(ref, ref, sem).wait()


PLACES = (
    (0, 0, 320), (1, 0, 320), (2, 0, 320), (3, 0, 320), (4, 0, 320), (5, 0, 320),
    (6, 0, 320), (7, 0, 320),
)

ORDER = (
    (
        ("e1", 0), ("e1b", 0), ("e1c", 0), ("panel_f1", 0), ("e1", 1), ("e2", 0), ("panel_f2", 0),
        ("e1b", 1), ("e1c", 1), ("e2", 1), ("e3", 0), ("e1", 2), ("panel_share", 0),
        ("panel_h", 0), ("e1b", 2), ("e1c", 2), ("e3", 1), ("e1", 3), ("e4", 0),
        ("panel_turn", 0), ("e2", 2), ("panel_h", 1), ("e1b", 3), ("e1c", 3), ("e4", 1),
        ("e5", 0), ("e2", 3), ("e5b", 0), ("e3", 2), ("e1", 4), ("panel_h", 2), ("e5", 1),
        ("e1b", 4), ("e1c", 4), ("e5b", 1), ("panel_h", 3), ("e3", 3), ("e1", 5), ("e4", 2),
        ("e6", 0), ("e2", 4), ("e6", 1), ("e1b", 5), ("e1c", 5), ("panel_h", 4), ("e4", 3),
        ("e5", 2), ("e2", 5), ("e7", 0), ("e5b", 2), ("e3", 4), ("e1", 6), ("e7", 1),
        ("panel_h", 5), ("e5", 3), ("e1b", 6), ("e1c", 6), ("e3", 5), ("e1", 7), ("e5b", 3),
        ("panel_h", 6), ("e6", 2), ("e4", 4), ("e2", 6), ("e1b", 7), ("e1c", 7), ("e4", 5),
        ("e6", 3), ("e2", 7), ("e7", 2), ("e3", 6), ("panel_h", 7), ("e5", 4), ("e5b", 4),
        ("e5", 5), ("e5b", 5), ("e7", 3), ("e3", 7), ("e4", 6), ("panel_share_h", 0), ("e6", 4),
        ("e6", 5), ("e4", 7), ("e5", 6), ("e5b", 6), ("e7", 4), ("e7", 5),
        ("e5b", 7), ("e5", 7), ("e6", 6), ("e6", 7), ("panel_join", 0), ("e7", 6), ("e7", 7),
    ),
    (
        ("bo", 0), ("bo", 1), ("bo", 2), ("bo", 3), ("bi", 0), ("bi", 1), ("bi", 2), ("bi", 3),
        ("outer", 0), ("outer", 1), ("outer", 2), ("outer", 3), ("outer", 4), ("u1", 0),
        ("outer", 5), ("u1b", 0), ("u1c", 0), ("outer", 6), ("u1", 1), ("outer", 7),
        ("outer_send", 0), ("right", 0), ("right", 1), ("u1b", 1), ("u1c", 1), ("u2", 0),
        ("right", 2), ("right", 3), ("right", 4), ("right", 5), ("right", 6), ("right", 7),
        ("l1", 0), ("u1", 2), ("u2", 1), ("u1b", 2), ("u1c", 2), ("u3", 0), ("l2", 0), ("u1", 3),
        ("u2", 2), ("u3", 1), ("u4", 0), ("u1b", 3), ("u1c", 3), ("l3", 0), ("u2", 3), ("u4", 1),
        ("u3", 2), ("l4", 0), ("u3", 3), ("u4", 2), ("u4", 3),
    ),
)


RingSum = collections.namedtuple(
    "RingSum", ("far", "near", "rest", "second", "third", "total", "sent")
)


def run(order, **stages):
    for name, k in order:
        stages[name](k)


def step_kernel(
    places, parts, order,
    grads, left, right, first, second, left_stats, right_stats,
    update_out, first_out, second_out, left_out, right_out,
    own, swap, ring, pair, cols, panel, panel_h, panel_t, panel_cat,
    basis, moment, square, turned, scaled, back_out, back, terms, terms_ring, halves, halves_out,
    outer, outer_swap, outer_ring, outer_pair, lstats, rstats, slice_t,
    load_sem, own_sem, swap_send, swap_recv, ring_send, ring_recv, pair_send, pair_recv,
    gather_send, gather_recv, panel_send, panel_recv, back_send, back_recv,
    terms_send, terms_recv, halves_send, halves_recv,
    outer_send, outer_recv, out_sem,
):
    dp = lax.axis_index("dp")
    mp = lax.axis_index("mp")
    z, yl, c = dp // 4, (dp // 2) % 2, dp % 2
    x, yh = mp // 2, mp % 2
    zn, zp, zo = (z + 1) % 4, (z + 3) % 4, (z + 2) % 4
    xn, xp, xo = (x + 1) % 4, (x + 3) % 4, (x + 2) % 4
    core_peer = {"dp": z * 4 + yl * 2 + (1 - c)}
    y_peer = {"dp": z * 4 + (1 - yl) * 2 + c}
    z_next = {"dp": zn * 4 + yl * 2 + c}
    z_prev = {"dp": zp * 4 + yl * 2 + c}
    h_peer = {"mp": x * 2 + (1 - yh)}
    q_peer = {"dp": z * 4 + (1 - yl) * 2 + c, "mp": x * 2 + (1 - yh)}
    x_next = {"mp": xn * 2 + yh}
    x_prev = {"mp": xp * 2 + yh}
    partners = (core_peer, y_peer, z_next, z_prev, h_peer, q_peer, x_next, x_prev)

    rows, width = own.shape[2], own.shape[3]
    chunks = own.shape[0]
    block = width * chunks
    half = rows // 2
    part = back.shape[2]
    hold = part * parts
    depth = panel.shape[2]

    def columns(owner, k):
        return pl.ds(pl.multiple_of(owner * block + k * width, 128), width)

    me = z * 2 + yl
    local_copy(left, panel.at[c, me], load_sem.at[0]).start()
    def piece(ref, i):
        k, lo, size = places[i]
        return ref.at[k, :, pl.ds(lo, size)]

    for i, (k, lo, size) in enumerate(places):
        for j in range(8):
            local_copy(
                grads.at[0, pl.ds(lo, size), columns(j * 2 + c, k)],
                own.at[k, j, pl.ds(lo, size)], own_sem.at[i],
            ).start()

    barrier = pltpu.get_barrier_semaphore()
    for p in partners:
        pl.semaphore_signal(barrier, inc=1, device_id=p, device_id_type=MESH)
    pl.semaphore_wait(barrier, len(partners))

    arrived(panel.at[0, 0], load_sem.at[0])

    def panel_copy(slot, n, **device):
        return remote_copy(
            panel.at[c, slot], panel.at[c, slot], panel_send.at[n], panel_recv.at[n], **device
        )

    panel_copy(me, 0, **y_peer).start()
    panel_copy(me, 1, **z_next).start()
    panel_copy(me, 2, **z_prev).start()

    for i, (k, lo, size) in enumerate(places):
        for j in range(8):
            remote_copy(
                grads.at[0, pl.ds(lo, size), columns(j * 2 + 1 - c, k)],
                swap.at[k, j, pl.ds(lo, size)],
                swap_send.at[i], swap_recv.at[i], **core_peer,
            ).start()

    local_copy(right.at[0], basis, load_sem.at[1]).start()
    local_copy(first, moment, load_sem.at[2]).start()
    local_copy(second, square, load_sem.at[3]).start()
    local_copy(left_stats, lstats, load_sem.at[4]).start()
    local_copy(right_stats.at[0], rstats, load_sem.at[5]).start()

    one = panel.at[0, 0]

    def panel_part(slot, lo, n, **device):
        piece = panel.at[c, slot, pl.ds(lo, depth // 2)]
        remote_copy(piece, piece, panel_send.at[n], panel_recv.at[n], **device).start()

    def panel_forward():
        arrived(one, panel_recv.at[1])
        panel_part(zp * 2 + yl, 0, 3, **z_next)
        panel_copy(zp * 2 + yl, 5, **y_peer).start()
        arrived(one, panel_recv.at[2])
        panel_part(zn * 2 + yl, depth // 2, 4, **z_prev)
        panel_copy(zn * 2 + yl, 6, **y_peer).start()

    def panel_forward_far():
        for n in (3, 4):
            arrived(panel.at[0, 0, pl.ds(0, depth // 2)], panel_recv.at[n])
        panel_copy(zo * 2 + yl, 17, **y_peer).start()

    def panel_share():
        for n in (0, 5, 6, 17):
            arrived(one, panel_recv.at[n])
        remote_copy(
            panel.at[c], panel.at[c], panel_send.at[7], panel_recv.at[7], **core_peer
        ).start()

    def panel_h_copy(j):
        remote_copy(
            panel.at[c, j], panel_h.at[c, j], panel_send.at[9 + j], panel_recv.at[9 + j], **q_peer
        ).start()

    def panel_turn():
        arrived(panel.at[0], panel_recv.at[7])
        for i in range(4):
            four = jnp.concatenate(
                [panel[0, 2 * i], panel[1, 2 * i], panel[0, 2 * i + 1], panel[1, 2 * i + 1]], axis=0
            )
            panel_t[:, pl.ds(i * 4 * depth, 4 * depth)] = four.T

    def panel_share_h():
        for j in range(8):
            arrived(panel.at[0, 0], panel_recv.at[9 + j])
        remote_copy(
            panel_h.at[c], panel_h.at[c], panel_send.at[8], panel_recv.at[8], **core_peer
        ).start()

    def panel_join():
        arrived(panel.at[0], panel_recv.at[8])

        def join(j, carry):
            for i in range(2):
                panel_cat[j, pl.ds(i * depth, depth)] = jnp.concatenate(
                    [panel[i, j], panel_h[i, j]], axis=1
                )
            return carry

        lax.fori_loop(0, 8, join, 0)

    def ring_stages(own, ring, send, recv, now, nxt, prv, opp, to_next, to_prev):
        def copy(j, slot, device):
            remote_copy(own.at[j], ring.at[slot], send.at[slot], recv.at[slot], **device).start()

        def far_stage(term):
            term(opp * 2)
            copy(opp * 2, 0, to_next)
            term(opp * 2 + 1)
            copy(opp * 2 + 1, 1, to_prev)

        def near_stage(term):
            term(nxt * 2 + 1)
            copy(nxt * 2 + 1, 3, to_next)
            term(prv * 2)
            copy(prv * 2, 4, to_prev)

        def rest_stage(term):
            term(nxt * 2)
            term(prv * 2 + 1)
            term(now * 2)
            term(now * 2 + 1)

        def second_stage():
            arrived(ring.at[0], recv.at[0])
            j = nxt * 2
            own[j] = (own[j].astype(F32) + ring[0].astype(F32)).astype(BF16)
            copy(j, 2, to_next)
            arrived(ring.at[1], recv.at[1])
            i = prv * 2 + 1
            own[i] = (own[i].astype(F32) + ring[1].astype(F32)).astype(BF16)
            copy(i, 5, to_prev)

        def third_stage():
            for slot in (3, 4, 2, 5):
                arrived(ring.at[slot], recv.at[slot])

        def total(which):
            return (
                own[now * 2 + which].astype(F32)
                + ring[2 + which].astype(F32)
                + ring[4 + which].astype(F32)
            )

        def sent():
            for slot in range(6):
                arrived(ring.at[slot], send.at[slot])

        return RingSum(far_stage, near_stage, rest_stage, second_stage, third_stage, total, sent)

    grad_rings = [
        ring_stages(
            piece(own, i), piece(ring, i), ring_send.at[i], ring_recv.at[i],
            z, zn, zp, zo, z_next, z_prev,
        )
        for i in range(len(places))
    ]

    def e1_term(i):
        mine, theirs = piece(own, i), piece(swap, i)

        def add(j):
            mine[j] = (mine[j].astype(F32) + theirs[j].astype(F32)).astype(BF16)

        return add

    def e1(i):
        arrived(piece(own, i), own_sem.at[i])
        arrived(piece(swap, i), swap_recv.at[i])
        grad_rings[i].far(e1_term(i))

    def e1b(i):
        grad_rings[i].near(e1_term(i))

    def e1c(i):
        grad_rings[i].rest(e1_term(i))

    def e2(i):
        grad_rings[i].second()

    def pair_piece(i):
        k, lo, size = places[i]
        return pair.at[k, pl.ds(lo, size)]

    def e3(i):
        grad_rings[i].third()
        mine = piece(own, i)
        j = z * 2 + 1 - yl
        mine[j] = grad_rings[i].total(1 - yl).astype(BF16)
        remote_copy(
            mine.at[j], pair_piece(i), pair_send.at[i], pair_recv.at[i], **y_peer
        ).start()

    def gather_piece(i, m, which=None):
        k, lo, size = places[i]
        if which is not None:
            size //= 2
            lo += which * size
        return cols.at[k, m, pl.ds(lo, size)]

    def gather_copy(i, m, n, which=None, **device):
        part = gather_piece(i, m, which)
        remote_copy(part, part, gather_send.at[i, n], gather_recv.at[i, n], **device).start()

    def gather_arrived(i, n):
        arrived(gather_piece(i, 0, None if n < 5 else 0), gather_recv.at[i, n])

    def e4(i):
        k, lo, size = places[i]
        arrived(pair_piece(i), pair_recv.at[i])
        cols[k, mp, pl.ds(lo, size)] = (
            grad_rings[i].total(yl) + pair_piece(i)[...].astype(F32)
        ).astype(BF16)
        gather_copy(i, mp, 0, **h_peer)
        gather_copy(i, mp, 1, **x_next)
        gather_copy(i, mp, 2, **x_prev)

    def e5b(i):
        gather_arrived(i, 0)
        gather_copy(i, x * 2 + 1 - yh, 3, **x_next)
        gather_copy(i, x * 2 + 1 - yh, 4, **x_prev)

    def e5(i):
        gather_arrived(i, 1)
        gather_copy(i, xp * 2 + yh, 5, 0, **x_next)
        gather_arrived(i, 2)
        gather_copy(i, xn * 2 + yh, 6, 1, **x_prev)

    def e6(i):
        gather_arrived(i, 3)
        gather_copy(i, xp * 2 + 1 - yh, 7, 0, **x_next)
        gather_arrived(i, 4)
        gather_copy(i, xn * 2 + 1 - yh, 8, 1, **x_prev)

    def e7(k):
        for i, place in enumerate(places):
            if place[0] == k:
                for n in (5, 6, 7, 8):
                    gather_arrived(i, n)
        rotated = jnp.dot(
            panel_t[...], cols[k].reshape(8 * rows, width), preferred_element_type=F32
        ).astype(BF16)
        if k == 0:
            arrived(basis, load_sem.at[1])
        for n in range(4):
            at = pl.ds(n * (block // 4), block // 4)
            term = jnp.dot(
                rotated, basis[pl.ds(k * width, width), at], preferred_element_type=F32
            )
            turned[:, at] = term if k == 0 else turned[:, at] + term

    run(
        order[0],
        e1=e1, e1b=e1b, e1c=e1c, e2=e2, e3=e3, e4=e4, e5=e5, e5b=e5b, e6=e6, e7=e7,
        panel_f1=lambda _: panel_forward(), panel_f2=lambda _: panel_forward_far(),
        panel_share=lambda _: panel_share(), panel_turn=lambda _: panel_turn(),
        panel_h=panel_h_copy, panel_share_h=lambda _: panel_share_h(),
        panel_join=lambda _: panel_join(),
    )

    arrived(moment, load_sem.at[2])
    arrived(square, load_sem.at[3])

    def moments(i, carry):
        at = pl.ds(pl.multiple_of(i * 32, 32), 32)
        t = turned[at]
        new_first = beta_first * moment[at] + (1.0 - beta_first) * t
        new_second = beta_second * square[at] + (1.0 - beta_second) * t * t
        moment[at] = new_first
        square[at] = new_second
        scaled[at] = (new_first / (jnp.sqrt(new_second) + epsilon)).astype(BF16)
        return carry

    lax.fori_loop(0, rows // 32, moments, 0)
    local_copy(moment, first_out, out_sem.at[0]).start()
    local_copy(square, second_out, out_sem.at[1]).start()

    def back_part(which, k):
        at = pl.ds(pl.multiple_of(which * hold + k * part, 128), part)
        return lax.dot_general(
            scaled[...], basis[at], (((1,), (1,)), ((), ())), preferred_element_type=F32
        ).astype(BF16)

    def back_send_part(k):
        back_out[k] = back_part(1 - yh, k)
        remote_copy(
            back_out.at[k], back.at[k, pl.ds(rows, rows)], back_send.at[k], back_recv.at[k],
            **h_peer,
        ).start()

    def back_keep_part(k):
        back[k, pl.ds(0, rows)] = back_part(yh, k)

    def outer_terms(j, carry):
        total = jnp.zeros((rows, rows), F32)
        for k in range(chunks):
            total += lax.dot_general(
                cols[k, j], cols[k, mp], (((1,), (1,)), ((), ())), preferred_element_type=F32
            )
        outer[0, j] = total[:half].astype(BF16)
        outer[1, j] = total[half:].astype(BF16)
        return carry

    def outer_part(i):
        lax.fori_loop(i, i + 1, outer_terms, 0)

    def outer_share():
        remote_copy(
            outer.at[1 - c], outer_swap, outer_send.at[6], outer_recv.at[6], **core_peer
        ).start()

    outer_rings = ring_stages(
        outer.at[c], outer_ring, outer_send, outer_recv, z, zn, zp, zo, z_next, z_prev
    )

    def l1():
        arrived(outer_swap, outer_recv.at[6])

        def add(j):
            outer[c, j] = (outer[c, j].astype(F32) + outer_swap[j].astype(F32)).astype(BF16)

        outer_rings.far(add)
        outer_rings.near(add)
        outer_rings.rest(add)

    def l2():
        outer_rings.second()

    def l3():
        outer_rings.third()
        j = z * 2 + 1 - yl
        outer[c, j] = outer_rings.total(1 - yl).astype(BF16)
        remote_copy(
            outer.at[c, j], outer_pair, outer_send.at[7], outer_recv.at[7], **y_peer
        ).start()

    def l4():
        arrived(outer_pair, outer_recv.at[7])
        arrived(lstats, load_sem.at[4])
        total = outer_rings.total(yl) + outer_pair[...].astype(F32)
        lstats[...] = beta_stats * lstats[...] + (1.0 - beta_stats) * total
        local_copy(lstats, left_out, out_sem.at[2]).start()

    def right_terms(k):
        if k == 0:
            share = rstats.shape[0]
            k_own = (mp * share) // width
            off = pl.ds(pl.multiple_of((mp * share) % width, 128), share)
            for i in range(4):
                two = cols[k_own, pl.ds(2 * i, 2), :, off].reshape(2 * rows, share)
                slice_t[:, pl.ds(i * 2 * rows, 2 * rows)] = two.T
            arrived(rstats, load_sem.at[5])
        at = pl.ds(k * width, width)
        term = jnp.dot(slice_t[...], cols[k].reshape(8 * rows, width), preferred_element_type=F32)
        rstats[:, at] = beta_stats * rstats[:, at] + (1.0 - beta_stats) * term
        if k == chunks - 1:
            local_copy(rstats, right_out.at[0], out_sem.at[3]).start()

    term_rings = [
        ring_stages(
            terms.at[k], terms_ring.at[k], terms_send.at[k], terms_recv.at[k],
            x, xn, xp, xo, x_next, x_prev,
        )
        for k in range(parts)
    ]

    def u1_term(k):
        def term(j):
            terms[k, j] = jnp.dot(
                panel_cat[j], back[k], preferred_element_type=F32
            ).astype(BF16)

        return term

    def u1(k):
        arrived(back.at[k, pl.ds(0, rows)], back_recv.at[k])
        term_rings[k].far(u1_term(k))

    def u1b(k):
        term_rings[k].near(u1_term(k))

    def u1c(k):
        term_rings[k].rest(u1_term(k))

    def u2(k):
        term_rings[k].second()

    def u3(k):
        term_rings[k].third()
        halves_out[k] = term_rings[k].total(1 - yh).astype(BF16)
        remote_copy(
            halves_out.at[k], halves.at[yh, k], halves_send.at[k], halves_recv.at[k], **h_peer
        ).start()
        halves[yh, k] = term_rings[k].total(yh).astype(BF16)
        local_copy(
            halves.at[yh, k],
            update_out.at[:, pl.ds(pl.multiple_of(yh * hold + k * part, 128), part)],
            out_sem.at[4],
        ).start()

    def u4(k):
        arrived(halves.at[0, k], halves_recv.at[k])
        local_copy(
            halves.at[1 - yh, k],
            update_out.at[:, pl.ds(pl.multiple_of((1 - yh) * hold + k * part, 128), part)],
            out_sem.at[5],
        ).start()

    run(
        order[1],
        bo=back_send_part, bi=back_keep_part, u1=u1, u1b=u1b, u1c=u1c, u2=u2, u3=u3, u4=u4,
        outer=outer_part, outer_send=lambda _: outer_share(),
        l1=lambda _: l1(), l2=lambda _: l2(), l3=lambda _: l3(), l4=lambda _: l4(),
        right=right_terms,
    )

    for n in (0, 1, 2, 5, 6, 17):
        arrived(panel.at[0, 0], panel_send.at[n])
    for n in (3, 4):
        arrived(panel.at[0, 0, pl.ds(0, depth // 2)], panel_send.at[n])
    for n in range(7, 9):
        arrived(panel.at[0], panel_send.at[n])
    for n in range(9, 17):
        arrived(panel.at[0, 0], panel_send.at[n])
    for i in range(len(places)):
        arrived(piece(swap, i), swap_send.at[i])
        grad_rings[i].sent()
        arrived(pair_piece(i), pair_send.at[i])
        for n in range(9):
            arrived(gather_piece(i, 0, None if n < 5 else 0), gather_send.at[i, n])
    for k in range(parts):
        arrived(back_out.at[k], back_send.at[k])
        term_rings[k].sent()
        arrived(halves_out.at[k], halves_send.at[k])
    outer_rings.sent()
    arrived(outer_swap, outer_send.at[6])
    arrived(outer_pair, outer_send.at[7])
    arrived(moment, out_sem.at[0])
    arrived(square, out_sem.at[1])
    arrived(lstats, out_sem.at[2])
    arrived(rstats, out_sem.at[3])
    arrived(halves.at[0], out_sem.at[4])
    arrived(halves.at[0], out_sem.at[5])


def hand_over(*refs):
    ins, outs, buffers, in_sems, out_sems = refs[:5], refs[5:10], refs[10:15], refs[15], refs[16]
    cuts = 4
    pieces = []
    for i in range(5):
        count = cuts if i < 3 else 1
        size = ins[i].shape[0] // count
        for n in range(count):
            at = pl.ds(n * size, size)
            pieces.append((i, n, at))
    for i, n, at in pieces:
        local_copy(ins[i].at[at], buffers[i].at[at], in_sems.at[i, n]).start()
    for i, n, at in pieces:
        arrived(buffers[i].at[at], in_sems.at[i, n])
        local_copy(buffers[i].at[at], outs[i].at[at], out_sems.at[i, n]).start()
    for i, n, at in pieces:
        arrived(buffers[i].at[at], out_sems.at[i, n])


def on_device(
    gradients, left_basis, right_basis, first_moment, second_moment, left_stats, right_stats,
    chunks=8, parts=4, places=PLACES, order=ORDER,
):
    rows, block = gradients.shape[1], gradients.shape[2] // 16
    width = block // chunks
    part = block // 2 // parts
    depth, span = left_basis.shape
    share = right_stats.shape[1]
    dma = pltpu.SemaphoreType.DMA
    any_space = pl.BlockSpec(memory_space=pl.ANY)

    def buffer(*shape, dtype=BF16):
        return pltpu.VMEM(shape, dtype)

    results = pl.pallas_call(
        functools.partial(step_kernel, places, parts, order),
        name="soap_step",
        out_shape=(
            jax.ShapeDtypeStruct((rows, block), BF16),
            jax.ShapeDtypeStruct((rows, block), F32),
            jax.ShapeDtypeStruct((rows, block), F32),
            jax.ShapeDtypeStruct((depth, span), F32),
            jax.ShapeDtypeStruct((1, share, block), F32),
        ),
        in_specs=[any_space] * 7,
        out_specs=(any_space,) * 5,
        scratch_shapes=[
            buffer(chunks, 8, rows, width),
            buffer(chunks, 8, rows, width),
            buffer(chunks, 6, rows, width),
            buffer(chunks, rows, width),
            buffer(chunks, 8, rows, width),
            buffer(2, 8, depth, span),
            buffer(2, 8, depth, span),
            buffer(span, 16 * depth),
            buffer(8, 2 * depth, 2 * span),
            buffer(block, block),
            buffer(rows, block, dtype=F32),
            buffer(rows, block, dtype=F32),
            buffer(rows, block, dtype=F32),
            buffer(rows, block),
            buffer(parts, rows, part),
            buffer(parts, 2 * rows, part),
            buffer(parts, 8, rows, part),
            buffer(parts, 6, rows, part),
            buffer(2, parts, rows, part),
            buffer(parts, rows, part),
            buffer(2, 8, depth, span),
            buffer(8, depth, span),
            buffer(6, depth, span),
            buffer(depth, span),
            buffer(depth, span, dtype=F32),
            buffer(share, block, dtype=F32),
            buffer(share, 8 * rows),
            dma((6,)),
            dma((len(places),)),
            dma((len(places),)),
            dma((len(places),)),
            dma((len(places), 6)),
            dma((len(places), 6)),
            dma((len(places),)),
            dma((len(places),)),
            dma((len(places), 9)),
            dma((len(places), 9)),
            dma((18,)),
            dma((18,)),
            dma((parts,)),
            dma((parts,)),
            dma((parts, 6)),
            dma((parts, 6)),
            dma((parts,)),
            dma((parts,)),
            dma((8,)),
            dma((8,)),
            dma((6,)),
        ],
        compiler_params=pltpu.CompilerParams(
            collective_id=0, has_side_effects=True, vmem_limit_bytes=62 * 1024 * 1024
        ),
    )(gradients, left_basis, right_basis, first_moment, second_moment, left_stats, right_stats)
    return pl.pallas_call(
        hand_over,
        name="hand_over",
        out_shape=tuple(jax.ShapeDtypeStruct(r.shape, r.dtype) for r in results),
        in_specs=[any_space] * 5,
        out_specs=(any_space,) * 5,
        scratch_shapes=[pltpu.VMEM(r.shape, r.dtype) for r in results] + [dma((5, 4)), dma((5, 4))],
    )(*results)


def solution(mesh):
    return jax.shard_map(
        on_device,
        mesh=mesh,
        in_specs=(
            P("dp", "mp", None),
            P("dp", "mp"),
            P("dp", None, None),
            P("mp", "dp"),
            P("mp", "dp"),
            P("dp", "mp"),
            P("dp", "mp", None),
        ),
        out_specs=(P("mp", "dp"), P("mp", "dp"), P("mp", "dp"), P("dp", "mp"), P("dp", "mp", None)),
        check_vma=False,
    )
```
